128 devices in a mesh: grp: 2 (over y_hi), ti: 8 (over x, y_lo), tj: 8 (over z, core).
Axes of the slice: x: 4, y: 4 (y_hi: 2, y_lo: 2; y = y_hi * 2 + y_lo), z: 4, core: 2. Of those that a mesh axis runs over, the one named last changes fastest.
Arguments:
- corpus: bfloat16 [2, 49152, 1024], P('grp', ('ti', 'tj')), may hold values from -64 to 64
- slot_of_row: int32 [2, 49152], P('grp', ('ti', 'tj')), may hold values from -1 to 49151, as said below
Outputs:
- max_similarity: float32 [2, 24576], P('grp', ('ti', 'tj'))
The draws below stay inside these ranges and needn't reach their ends.
Inputs may be any that keep to these rules, and one draw needn't show every extreme that they name: `slot_of_row`: every value from 0 to 49151 appears exactly once; a row with value v lies on a device whose ti index is (v % 24576) // 3072; from one device at most 48 rows have values in one aligned group of 384 consecutive values, and some device sends exactly 48 to some group.
All inputs are finite; a program needn't handle non-finite values.
Results may differ from the reference program's by a relative error of at most 0.0009.
Values may be sent and summed in bfloat16 or wider, within the bound.
No kernel may reach another device: no remote copies, remote signals or barrier semaphores. Data moves between devices by JAX's collectives and lax.ppermute only.
A program may use at most 64 MiB of HBM per device.

```python
import jax
import jax.numpy as jnp
from jax import lax

D = 1024
BLK = 3072
GROUPS = 2
SUB_ROWS = 384
CAP = 48
SRC_DEV = 768
CLUSTER = 24576
GRID_ROWS = 49152


def slot_table(key):
    lane_count = BLK // SUB_ROWS
    owners = 2 * lane_count
    average = CAP // 2
    key_list = jax.random.split(jax.random.fold_in(key, 11), 4)
    swings = jax.random.randint(key_list[0], (lane_count, lane_count), -average, average + 1)
    swings = swings.at[:, 0].set(average)
    paired = jnp.stack([average + swings, average - swings], axis=2).reshape(lane_count, owners)
    orders = jax.vmap(lambda sub_key: jax.random.permutation(sub_key, owners))(jax.random.split(key_list[1], lane_count))
    shares = jnp.take_along_axis(paired, orders, axis=1)
    sender = jnp.arange(owners)
    offsets = (sender[None, :] - sender[:, None]) % owners
    counts = shares[:, offsets]
    ends = jnp.cumsum(counts, axis=2)
    starts = ends - counts
    members = jnp.arange(SUB_ROWS)
    target = jnp.sum((members[None, None, :, None] >= ends[:, :, None, :]).astype(jnp.int32), axis=3)
    within = members[None, None, :] - jnp.take_along_axis(starts, target, axis=2)
    arrival = jnp.cumsum(counts, axis=1) - counts
    position = jnp.take_along_axis(arrival, target, axis=2) + within
    shuffles = jax.vmap(lambda sub_key: jax.random.permutation(sub_key, SUB_ROWS))(jax.random.split(key_list[2], lane_count * owners))
    shuffles = shuffles.reshape(lane_count, owners * SUB_ROWS)
    lookup = (target * SUB_ROWS + position).reshape(lane_count, owners * SUB_ROWS)
    placed = jnp.take_along_axis(shuffles, lookup, axis=1).reshape(lane_count, owners, SUB_ROWS)
    row_index = jnp.arange(lane_count)[:, None, None]
    values = target // lane_count * CLUSTER + row_index * BLK + target % lane_count * SUB_ROWS + placed
    local_rows = jax.vmap(lambda sub_key: jax.random.permutation(sub_key, SRC_DEV))(jax.random.split(key_list[3], lane_count * owners))[:, :SUB_ROWS]
    table = jax.vmap(lambda spots, entries: jnp.full((SRC_DEV,), -1, jnp.int32).at[spots].set(entries.astype(jnp.int32)))(local_rows, values.reshape(lane_count * owners, SUB_ROWS))
    table = table.reshape(lane_count, 2, lane_count, SRC_DEV).transpose(1, 0, 2, 3).reshape(2, lane_count * lane_count * SRC_DEV)
    return table.astype(jnp.int32)


def draw_slot_of_row(key, part):
    return slot_table(key)


def draw_corpus(key, part):
    table = slot_table(key)
    total = 2 * CLUSTER
    key_list = jax.random.split(jax.random.fold_in(key, 23), 9)
    basis = jax.random.normal(key_list[0], (total, D), jnp.float32)
    partner = jnp.concatenate([jax.random.permutation(key_list[1], CLUSTER), CLUSTER + jax.random.permutation(key_list[2], CLUSTER)])
    strong = jax.random.randint(key_list[3], (total,), 0, 4) == 0
    mixing = jnp.where(strong, jax.random.uniform(key_list[4], (total,), jnp.float32, 1.0, 4.0), jax.random.uniform(key_list[5], (total,), jnp.float32, 0.0, 0.3))
    cluster_rows = basis + mixing[:, None] * basis[partner]
    filler = jax.random.normal(key_list[8], (2, GRID_ROWS, D), jnp.float32)
    chosen = cluster_rows[jnp.clip(table, 0, total - 1)]
    result = jnp.where((table >= 0)[..., None], chosen, filler)
    return jnp.clip(result, -64.0, 64.0).astype(jnp.bfloat16)


def setup_inputs(seed: int = 0) -> dict:
    streams_of = jax.random.split(jax.random.key(seed), 3)
    return {
        "corpus": draw_corpus(jax.random.fold_in(streams_of[2], 71), 0),
        "slot_of_row": draw_slot_of_row(jax.random.fold_in(streams_of[2], 71), 0),
    }


epsilon = 1e-06

def reference(corpus, slot_of_row):
    features = corpus.shape[2]
    flat_rows = corpus.reshape(-1, features)
    slots = slot_of_row.reshape(-1).astype(jnp.int32)
    total = GROUPS * CLUSTER
    target = jnp.where(slots >= 0, slots, total).astype(jnp.int32)
    cluster_rows = jnp.zeros((total, features), corpus.dtype).at[target].set(flat_rows, mode='drop')
    widened = cluster_rows.astype(jnp.float32)
    row_squares = lax.optimization_barrier(jnp.sum(widened * widened, axis=1, keepdims=True))
    inverse_norm = lax.rsqrt(row_squares + epsilon)
    unit_rows = (widened * inverse_norm).astype(jnp.bfloat16)
    per_group = CLUSTER // BLK

    def one_block(pair_index):
        group_start = pair_index // per_group * CLUSTER
        local_start = pair_index % per_group * BLK
        queries = lax.dynamic_slice_in_dim(unit_rows, (group_start + local_start).astype(jnp.int32), BLK, 0)
        members = lax.dynamic_slice_in_dim(unit_rows, group_start.astype(jnp.int32), CLUSTER, 0)
        scores = jnp.dot(queries, members.T, preferred_element_type=jnp.float32)
        same = (local_start + jnp.arange(BLK, dtype=jnp.int32))[:, None] == jnp.arange(CLUSTER, dtype=jnp.int32)[None, :]
        scores = jnp.where(same, -2.0, scores)
        return lax.optimization_barrier(jnp.max(scores, axis=1))
    best = lax.map(one_block, jnp.arange(GROUPS * per_group, dtype=jnp.int32))
    return best.reshape(GROUPS, CLUSTER)
```

```python
import jax
import jax.numpy as jnp
from jax import lax
from jax.sharding import PartitionSpec as P

BLK = 3072
epsilon = 1e-06


def per_device(corpus, slot_of_row):
    rows_in = corpus[0]
    values = slot_of_row[0]
    src_count, features = rows_in.shape
    lanes = lax.axis_size("tj")
    sub_rows = src_count // 2
    cluster = BLK * lax.axis_size("ti")
    capacity = BLK // (lanes * lanes)
    owners = 2 * lanes
    tile_col = lax.axis_index("tj")

    widened = rows_in.astype(jnp.float32)
    row_squares = jnp.sum(widened * widened, axis=1, keepdims=True)
    unit = (widened * lax.rsqrt(row_squares + epsilon)).astype(jnp.bfloat16)

    member = values >= 0
    inside = values % cluster
    owner_of = jnp.where(member, values // cluster * lanes + inside % BLK // sub_rows, owners)
    position = inside % sub_rows
    onehot = owner_of[:, None] == jnp.arange(owners, dtype=jnp.int32)[None, :]
    index = jnp.arange(src_count, dtype=jnp.int32)
    before = (index[None, :] < index[:, None]).astype(jnp.bfloat16)
    ranks = jnp.dot(before, onehot.astype(jnp.bfloat16), preferred_element_type=jnp.float32)
    rank = jnp.sum(jnp.where(onehot, ranks, 0.0), axis=1).astype(jnp.int32)
    slot = jnp.where(member, owner_of * capacity + rank, owners * capacity)
    lane = jnp.arange(128, dtype=jnp.int32)[None, :]
    tags = jnp.where(
        lane == 0,
        (position // 16)[:, None],
        jnp.where(lane == 1, (position % 16)[:, None], jnp.where(lane == 2, 1, 0)),
    ).astype(jnp.bfloat16)
    pick = (slot[None, :] == jnp.arange(owners * capacity, dtype=jnp.int32)[:, None]).astype(jnp.bfloat16)
    send = jnp.dot(
        pick, jnp.concatenate([unit, tags], axis=1), preferred_element_type=jnp.float32
    ).astype(jnp.bfloat16)
    got = lax.all_to_all(
        send.reshape(owners, capacity, features + 128), ("grp", "tj"), 0, 0, tiled=True
    ).reshape(owners * capacity, features + 128)
    weights = jnp.where(lane == 0, 16.0, jnp.where(lane == 1, 1.0, jnp.where(lane == 2, 1.0, 0.0)))
    code = lax.dot_general(
        weights.astype(jnp.bfloat16),
        got[:, features:],
        (((1,), (1,)), ((), ())),
        preferred_element_type=jnp.float32,
    )
    place = (
        code.astype(jnp.int32) == jnp.arange(1, sub_rows + 1, dtype=jnp.int32)[:, None]
    ).astype(jnp.bfloat16)
    own = jnp.dot(place, got[:, :features], preferred_element_type=jnp.float32).astype(jnp.bfloat16)

    rows = lax.all_gather(own, "tj", axis=0, tiled=True)

    size = lax.axis_size("ti")
    up = [(i, (i + 2) % size) for i in range(size)]
    down = [(i, (i - 2) % size) for i in range(size)]
    across = [(i, i ^ 1) for i in range(size)]
    half = sub_rows // 2

    def send_to(value, pairs):
        return lax.ppermute(value, "ti", pairs)

    beside = send_to(own, across)
    from_low = send_to(own, up)
    from_high = send_to(own, down)
    far_top = send_to(from_low[:half], up)
    far_bottom = send_to(from_high[half:], down)
    beside_low = send_to(beside, up)
    beside_high = send_to(beside, down)
    far = jnp.concatenate([far_top, far_bottom], axis=0)
    beside_far = send_to(far, across)

    def best_of(columns, masked):
        scores = lax.dot_general(
            rows, columns, (((1,), (1,)), ((), ())), preferred_element_type=jnp.float32
        )
        if masked:
            row_slot = jnp.arange(BLK, dtype=jnp.int32)[:, None] - tile_col * sub_rows
            col_slot = jnp.arange(columns.shape[0], dtype=jnp.int32)[None, :]
            scores = jnp.where((row_slot == col_slot) & (col_slot < sub_rows), -2.0, scores)
        return jnp.max(scores, axis=1)

    best = best_of(jnp.concatenate([own, beside], axis=0), True)
    best = jnp.maximum(best, best_of(jnp.concatenate([from_low, from_high], axis=0), False))
    best = jnp.maximum(best, best_of(jnp.concatenate([far, beside_far], axis=0), False))
    best = jnp.maximum(best, best_of(jnp.concatenate([beside_low, beside_high], axis=0), False))
    parts = lax.all_to_all(best.reshape(lanes, sub_rows), "tj", 0, 0, tiled=True)
    return jnp.max(parts, axis=0)[None, :]


def solution(mesh):
    in_specs = (P("grp", ("ti", "tj"), None), P("grp", ("ti", "tj")))
    out_specs = P("grp", ("ti", "tj"))
    return jax.shard_map(
        per_device, mesh=mesh, in_specs=in_specs, out_specs=out_specs, check_vma=False
    )
```

```python
import functools

import jax
import jax.numpy as jnp
from jax import lax
from jax.experimental import pallas as pl
from jax.experimental.pallas import tpu as pltpu
from jax.sharding import PartitionSpec as P

BLK = 3072
SUB = 384
CHUNK = 256
epsilon = 1e-06


def start_copies(refs, groups, target, sems):
    copies, used = [], 0
    for slot, pieces in enumerate(groups):
        offset, slot_copies = 0, []
        for _ in range(pieces):
            ref = refs[used]
            height = ref.shape[0]
            slot_copies.append(
                pltpu.make_async_copy(ref, target.at[pl.ds(slot * SUB + offset, height)], sems.at[used])
            )
            slot_copies[-1].start()
            offset += height
            used += 1
        copies.append(slot_copies)
    return copies


def score_chunk(row_tile, cols, start, width):
    return lax.dot_general(
        row_tile,
        cols[pl.ds(start, width), :],
        (((1,), (1,)), ((), ())),
        preferred_element_type=jnp.float32,
    )


def chunks_of(total):
    return [(start, min(CHUNK, total - start)) for start in range(0, total, CHUNK)]


def fold(best, scores):
    for lane in range(0, scores.shape[1], 128):
        piece = scores[:, lane : lane + 128]
        best = piece if best is None else jnp.maximum(best, piece)
    return best


def maxima_kernel(groups, cols_count, masked, last, *refs):
    pieces = sum(groups)
    row_refs, refs = refs[:pieces], refs[pieces:]
    col_refs, refs = refs[:cols_count], refs[cols_count:]
    if last:
        first, second, row_out, col_out, rows, cols, row_sems, col_sems = refs
        col_out[...] = jnp.full(col_out.shape, -2.0, jnp.float32)
    else:
        row_out, rows, cols, row_sems, col_sems = refs
    col_copies = start_copies(col_refs, [1] * cols_count, cols, col_sems)
    row_copies = start_copies(row_refs, groups, rows, row_sems)
    for copies in col_copies + row_copies:
        for copy in copies:
            copy.wait()

    def do_block(index, best):
        row_tile = rows[pl.ds(pl.multiple_of(index * SUB, SUB), SUB), :]
        for start, width in chunks_of(cols_count * SUB):
            scores = score_chunk(row_tile, cols, start, width)
            if masked and start < SUB:
                row_at = lax.broadcasted_iota(jnp.int32, scores.shape, 0)
                col_at = lax.broadcasted_iota(jnp.int32, scores.shape, 1) + start + index * BLK
                scores = jnp.where(row_at == col_at, -2.0, scores)
            if last and start < 2 * SUB:
                col_out[:, pl.ds(start, width)] = jnp.maximum(
                    col_out[:, pl.ds(start, width)], jnp.max(scores, axis=0, keepdims=True)
                )
            best = fold(best, scores)
        return best

    if not last:

        @pl.loop(0, len(groups))
        def _(index):
            row_out[index] = do_block(index, None)

    else:

        @pl.loop(0, 6)
        def _(index):
            row_out[index] = jnp.max(do_block(index, first[index]).T, axis=0, keepdims=True)

        @pl.loop(6, 8)
        def _(index):
            row_out[index] = jnp.max(do_block(index, second[index - 6]).T, axis=0, keepdims=True)


def call_maxima(row_groups, columns, masked, earlier):
    groups = [len(group) for group in row_groups]
    flat = [piece for group in row_groups for piece in group]
    count, width = len(groups), columns[0].shape[1]
    last = bool(earlier)
    anywhere = pl.BlockSpec(memory_space=pl.ANY)
    whole = pl.BlockSpec(memory_space=pltpu.VMEM)
    if last:
        out_shape = (
            jax.ShapeDtypeStruct((count, 1, SUB), jnp.float32),
            jax.ShapeDtypeStruct((1, 2 * SUB), jnp.float32),
        )
        out_specs = (whole, whole)
    else:
        out_shape = jax.ShapeDtypeStruct((count, SUB, 128), jnp.float32)
        out_specs = whole
    rows_total, cols_total = count * SUB, len(columns) * SUB
    return pl.pallas_call(
        functools.partial(maxima_kernel, groups, len(columns), masked, last),
        out_shape=out_shape,
        in_specs=[anywhere] * (len(flat) + len(columns)) + [whole] * len(earlier),
        out_specs=out_specs,
        scratch_shapes=[
            pltpu.VMEM((rows_total, width), jnp.bfloat16),
            pltpu.VMEM((cols_total, width), jnp.bfloat16),
            pltpu.SemaphoreType.DMA((len(flat),)),
            pltpu.SemaphoreType.DMA((len(columns),)),
        ],
        cost_estimate=pl.CostEstimate(
            flops=2 * rows_total * cols_total * width,
            bytes_accessed=2 * (rows_total + cols_total) * width,
            transcendentals=0,
        ),
        compiler_params=pltpu.CompilerParams(vmem_limit_bytes=32 * 2**20),
    )(*flat, *columns, *earlier)


def tile_maxima(row_groups, columns, masked):
    return call_maxima(row_groups, columns, masked, ())


def last_maxima(row_groups, columns, first, second):
    row_best, col_best = call_maxima(row_groups, columns, False, (first, second))
    return row_best[:, 0, :], col_best.reshape(2, SUB)


def per_device(corpus, slot_of_row):
    rows_in = corpus[0]
    values = slot_of_row[0]
    src_count, features = rows_in.shape
    lanes = lax.axis_size("tj")
    sub_rows = src_count // 2
    cluster = BLK * lax.axis_size("ti")
    capacity = BLK // (lanes * lanes)
    owners = 2 * lanes
    tile_col = lax.axis_index("tj")

    widened = rows_in.astype(jnp.float32)
    row_squares = jnp.sum(widened * widened, axis=1, keepdims=True)
    unit = (widened * lax.rsqrt(row_squares + epsilon)).astype(jnp.bfloat16)

    member = values >= 0
    inside = values % cluster
    owner_of = jnp.where(member, values // cluster * lanes + inside % BLK // sub_rows, owners)
    position = inside % sub_rows
    onehot = owner_of[:, None] == jnp.arange(owners, dtype=jnp.int32)[None, :]
    index = jnp.arange(src_count, dtype=jnp.int32)
    before = (index[None, :] < index[:, None]).astype(jnp.bfloat16)
    ranks = jnp.dot(before, onehot.astype(jnp.bfloat16), preferred_element_type=jnp.float32)
    rank = jnp.sum(jnp.where(onehot, ranks, 0.0), axis=1).astype(jnp.int32)
    slot = jnp.where(member, owner_of * capacity + rank, owners * capacity)
    lane = jnp.arange(128, dtype=jnp.int32)[None, :]
    tags = jnp.where(
        lane == 0,
        (position // 16)[:, None],
        jnp.where(lane == 1, (position % 16)[:, None], jnp.where(lane == 2, 1, 0)),
    ).astype(jnp.bfloat16)
    pick = (slot[None, :] == jnp.arange(owners * capacity, dtype=jnp.int32)[:, None]).astype(jnp.bfloat16)
    send = jnp.dot(
        pick, jnp.concatenate([unit, tags], axis=1), preferred_element_type=jnp.float32
    ).astype(jnp.bfloat16)
    got = lax.all_to_all(
        send.reshape(owners, capacity, features + 128), ("grp", "tj"), 0, 0, tiled=True
    ).reshape(owners * capacity, features + 128)
    weights = jnp.where(lane == 0, 16.0, jnp.where(lane == 1, 1.0, jnp.where(lane == 2, 1.0, 0.0)))
    code = lax.dot_general(
        weights.astype(jnp.bfloat16),
        got[:, features:],
        (((1,), (1,)), ((), ())),
        preferred_element_type=jnp.float32,
    )
    place = (
        code.astype(jnp.int32) == jnp.arange(1, sub_rows + 1, dtype=jnp.int32)[:, None]
    ).astype(jnp.bfloat16)
    own = jnp.dot(place, got[:, :features], preferred_element_type=jnp.float32).astype(jnp.bfloat16)

    def along_rows(value, pairs):
        return lax.ppermute(value, "ti", pairs)

    def along_cols(value, pairs):
        return lax.ppermute(value, "tj", pairs)

    size = lax.axis_size("ti")
    up = [(i, (i + 2) % size) for i in range(size)]
    down = [(i, (i - 2) % size) for i in range(size)]
    far = [(i, (i + 4) % size) for i in range(size)]
    swap = [(i, i ^ 1) for i in range(size)]
    half = sub_rows // 2

    twin = along_cols(own, swap)
    beside = along_rows(own, swap)
    across = along_rows(own, far)
    low = along_cols(own, up)
    high = along_cols(own, down)

    low_twin = along_cols(low, swap)
    high_twin = along_cols(high, swap)
    after = along_rows(own, down)
    beside_before = along_rows(beside, up)
    beside_across = along_rows(across, swap)
    mid_top = along_cols(low[:half], up)
    mid_bottom = along_cols(high[half:], down)
    mid_top_twin = along_cols(mid_top, swap)
    mid_bottom_twin = along_cols(mid_bottom, swap)

    first = tile_maxima([[own], [twin], [low], [low_twin], [high], [high_twin]], [own, beside, across], True)
    second = tile_maxima([[mid_top, mid_bottom], [mid_top_twin, mid_bottom_twin]], [own, beside, across], False)
    row_best, col_best = last_maxima(
        [[own], [twin], [low], [low_twin], [high], [high_twin], [mid_top, mid_bottom], [mid_top_twin, mid_bottom_twin]],
        [after, beside_before, beside_across],
        first,
        second,
    )
    depth = lanes // 2
    order = jnp.array([0, 2, 3, 1], jnp.int32)
    target = jnp.arange(lanes, dtype=jnp.int32)
    distance = (target // 2 - tile_col // 2) % depth
    source = order[distance] * 2 + (target % 2) ^ (tile_col % 2)
    chosen = source[:, None] == target[None, :]
    outgoing = jnp.max(jnp.where(chosen[:, :, None], row_best[None], -2.0), axis=1)
    parts = lax.all_to_all(outgoing, "tj", 0, 0, tiled=True)
    from_before = along_rows(col_best[:1], up)
    from_beside = along_rows(col_best[1:], [(i, ((i ^ 1) - 2) % size) for i in range(size)])
    best = jnp.maximum(jnp.max(parts, axis=0), jnp.maximum(from_before[0], from_beside[0]))
    return best[None, :]


def solution(mesh):
    in_specs = (P("grp", ("ti", "tj"), None), P("grp", ("ti", "tj")))
    out_specs = P("grp", ("ti", "tj"))
    return jax.shard_map(
        per_device, mesh=mesh, in_specs=in_specs, out_specs=out_specs, check_vma=False
    )
```

```python
import functools

import jax
import jax.numpy as jnp
from jax import lax
from jax.experimental import pallas as pl
from jax.experimental.pallas import tpu as pltpu
from jax.sharding import PartitionSpec as P

BLK = 3072
SUB = 384
PAIR = 2 * SUB
CHUNK = 256
epsilon = 1e-06


def score_chunk(row_tile, cols, start, width):
    return lax.dot_general(
        row_tile,
        cols[pl.ds(start, width), :],
        (((1,), (1,)), ((), ())),
        preferred_element_type=jnp.float32,
    )


def maxima_kernel(row_count, col_count, plan, *refs):
    row_refs, refs = refs[:row_count], refs[row_count:]
    col_refs, refs = refs[:col_count], refs[col_count:]
    earlier_rows = earlier_cols = col_out = None
    if plan["earlier_rows"]:
        earlier_rows, refs = refs[0], refs[1:]
    if plan["earlier_cols"]:
        earlier_cols, refs = refs[0], refs[1:]
    row_out, refs = refs[0], refs[1:]
    traced = plan["traced"]
    if traced:
        col_out, refs = refs[0], refs[1:]
    rows, cols, row_sems, col_sems = refs

    def row_copy(block, ref):
        return pltpu.make_async_copy(ref, rows.at[pl.ds(block * SUB, SUB)], row_sems.at[block])

    col_copies = [
        pltpu.make_async_copy(ref, cols.at[pl.ds(block * SUB, SUB)], col_sems.at[block])
        for block, ref in enumerate(col_refs)
    ]
    row_copies = [row_copy(block, ref) for block, ref in enumerate(row_refs)]
    for copy in col_copies + row_copies:
        copy.start()
    if traced:
        col_out[...] = earlier_cols[...] if plan["earlier_cols"] else jnp.full(col_out.shape, -2.0, jnp.float32)
    for copy in col_copies:
        copy.wait()

    @pl.loop(0, row_count // 2)
    def _(index):
        for part in range(2):
            row_copy(index * 2 + part, row_refs[0]).wait()
        row_tile = rows[pl.ds(pl.multiple_of(index * PAIR, PAIR), PAIR), :]
        best = earlier_rows[index] if plan["earlier_rows"] else None
        for start in range(0, col_count * SUB, CHUNK):
            width = min(CHUNK, col_count * SUB - start)
            scores = score_chunk(row_tile, cols, start, width)
            if plan["masked"] and start < SUB:
                row_at = lax.broadcasted_iota(jnp.int32, scores.shape, 0)
                col_at = lax.broadcasted_iota(jnp.int32, scores.shape, 1) + (start + index * BLK)
                scores = jnp.where((row_at == col_at) & (col_at < SUB + index * BLK), -2.0, scores)
            if start < traced * SUB:
                col_out[:, pl.ds(start, width)] = jnp.maximum(
                    col_out[:, pl.ds(start, width)], jnp.max(scores, axis=0, keepdims=True)
                )
            for lane in range(0, width, 128):
                piece = scores[:, lane : lane + 128]
                best = piece if best is None else jnp.maximum(best, piece)
        row_out[index] = jnp.max(best.T, axis=0, keepdims=True) if plan["folded"] else best


def tile_maxima(row_blocks, columns, earlier_rows=None, earlier_cols=None, masked=False, folded=False, traced=0):
    plan = dict(
        earlier_rows=earlier_rows is not None,
        earlier_cols=earlier_cols is not None,
        masked=masked,
        folded=folded,
        traced=traced,
    )
    row_count, col_count, width = len(row_blocks), len(columns), columns[0].shape[1]
    pairs = row_count // 2
    anywhere = pl.BlockSpec(memory_space=pl.ANY)
    whole = pl.BlockSpec(memory_space=pltpu.VMEM)
    out_shape = [jax.ShapeDtypeStruct((pairs, 1, PAIR) if folded else (pairs, PAIR, 128), jnp.float32)]
    if traced:
        out_shape.append(jax.ShapeDtypeStruct((1, traced * SUB), jnp.float32))
    extra = [value for value in (earlier_rows, earlier_cols) if value is not None]
    return pl.pallas_call(
        functools.partial(maxima_kernel, row_count, col_count, plan),
        out_shape=out_shape,
        in_specs=[anywhere] * (row_count + col_count) + [whole] * len(extra),
        out_specs=[whole] * len(out_shape),
        scratch_shapes=[
            pltpu.VMEM((row_count * SUB, width), jnp.bfloat16),
            pltpu.VMEM((col_count * SUB, width), jnp.bfloat16),
            pltpu.SemaphoreType.DMA((row_count,)),
            pltpu.SemaphoreType.DMA((col_count,)),
        ],
        cost_estimate=pl.CostEstimate(
            flops=2 * row_count * col_count * SUB * SUB * width,
            bytes_accessed=2 * (row_count + col_count) * SUB * width,
            transcendentals=0,
        ),
        compiler_params=pltpu.CompilerParams(vmem_limit_bytes=20 * 2**20),
    )(*row_blocks, *columns, *extra)


def per_device(corpus, slot_of_row):
    rows_in = corpus[0]
    values = slot_of_row[0]
    src_count, features = rows_in.shape
    lanes = lax.axis_size("tj")
    sub_rows = src_count // 2
    cluster = BLK * lax.axis_size("ti")
    capacity = BLK // (lanes * lanes)
    owners = 2 * lanes
    tile_col = lax.axis_index("tj")

    widened = rows_in.astype(jnp.float32)
    row_squares = jnp.sum(widened * widened, axis=1, keepdims=True)
    unit = (widened * lax.rsqrt(row_squares + epsilon)).astype(jnp.bfloat16)

    member = values >= 0
    inside = values % cluster
    owner_of = jnp.where(member, values // cluster * lanes + inside % BLK // sub_rows, owners)
    position = inside % sub_rows
    onehot = owner_of[:, None] == jnp.arange(owners, dtype=jnp.int32)[None, :]
    index = jnp.arange(src_count, dtype=jnp.int32)
    before = (index[None, :] < index[:, None]).astype(jnp.bfloat16)
    ranks = jnp.dot(before, onehot.astype(jnp.bfloat16), preferred_element_type=jnp.float32)
    rank = jnp.sum(jnp.where(onehot, ranks, 0.0), axis=1).astype(jnp.int32)
    slot = jnp.where(member, owner_of * capacity + rank, owners * capacity)
    lane = jnp.arange(128, dtype=jnp.int32)[None, :]
    tags = jnp.where(
        lane == 0,
        (position // 16)[:, None],
        jnp.where(lane == 1, (position % 16)[:, None], jnp.where(lane == 2, 1, 0)),
    ).astype(jnp.bfloat16)
    pick = (slot[None, :] == jnp.arange(owners * capacity, dtype=jnp.int32)[:, None]).astype(jnp.bfloat16)
    send = jnp.dot(
        pick, jnp.concatenate([unit, tags], axis=1), preferred_element_type=jnp.float32
    ).astype(jnp.bfloat16)
    got = lax.all_to_all(
        send.reshape(owners, capacity, features + 128), ("grp", "tj"), 0, 0, tiled=True
    ).reshape(owners * capacity, features + 128)
    weights = jnp.where(lane == 0, 16.0, jnp.where(lane == 1, 1.0, jnp.where(lane == 2, 1.0, 0.0)))
    code = lax.dot_general(
        weights.astype(jnp.bfloat16),
        got[:, features:],
        (((1,), (1,)), ((), ())),
        preferred_element_type=jnp.float32,
    )
    place = (
        code.astype(jnp.int32) == jnp.arange(1, sub_rows + 1, dtype=jnp.int32)[:, None]
    ).astype(jnp.bfloat16)
    own = jnp.dot(place, got[:, :features], preferred_element_type=jnp.float32).astype(jnp.bfloat16)

    def along_rows(value, pairs):
        return lax.ppermute(value, "ti", pairs)

    def along_cols(value, pairs):
        return lax.ppermute(value, "tj", pairs)

    size = lax.axis_size("ti")
    up = [(i, (i + 2) % size) for i in range(size)]
    down = [(i, (i - 2) % size) for i in range(size)]
    far = [(i, (i + 4) % size) for i in range(size)]
    swap = [(i, i ^ 1) for i in range(size)]
    twin = along_cols(own, swap)
    beside = along_rows(own, swap)
    across = along_rows(own, far)
    low = along_cols(own, up)
    high = along_cols(own, down)

    later, low, high, beside, across = lax.optimization_barrier((own, low, high, beside, across))
    low_twin = along_cols(low, swap)
    high_twin = along_cols(high, swap)
    mid = along_cols(later, far)
    after = along_rows(later, down)
    beside_before = along_rows(beside, up)
    beside_across = along_rows(across, swap)

    near = [own, twin, low, low_twin, high, high_twin]
    (near_lanes,) = tile_maxima(near, [own, beside, across], masked=True)
    mid, near_lanes = lax.optimization_barrier((mid, near_lanes))
    mid_twin = along_cols(mid, swap)
    near_best, col_near = tile_maxima(
        near, [after, beside_before, beside_across], earlier_rows=near_lanes, folded=True, traced=2
    )
    mid_best, col_best = tile_maxima(
        [mid, mid_twin],
        [after, beside_before, own, beside, across, beside_across],
        earlier_cols=col_near,
        folded=True,
        traced=2,
    )
    row_best = jnp.concatenate([near_best.reshape(6, sub_rows), mid_best.reshape(2, sub_rows)], axis=0)
    col_best = col_best.reshape(2, sub_rows)
    depth = lanes // 2
    order = jnp.array([0, 2, 3, 1], jnp.int32)
    target = jnp.arange(lanes, dtype=jnp.int32)
    distance = (target // 2 - tile_col // 2) % depth
    source = order[distance] * 2 + (target % 2) ^ (tile_col % 2)
    chosen = source[:, None] == target[None, :]
    outgoing = jnp.max(jnp.where(chosen[:, :, None], row_best[None], -2.0), axis=1)
    parts = lax.all_to_all(outgoing, "tj", 0, 0, tiled=True)
    from_before = along_rows(col_best[:1], up)
    from_beside = along_rows(col_best[1:], [(i, ((i ^ 1) - 2) % size) for i in range(size)])
    best = jnp.maximum(jnp.max(parts, axis=0), jnp.maximum(from_before[0], from_beside[0]))
    return best[None, :]


def solution(mesh):
    in_specs = (P("grp", ("ti", "tj"), None), P("grp", ("ti", "tj")))
    out_specs = P("grp", ("ti", "tj"))
    return jax.shard_map(
        per_device, mesh=mesh, in_specs=in_specs, out_specs=out_specs, check_vma=False
    )
```

```python
import functools

import jax
import jax.numpy as jnp
from jax import lax
from jax.experimental import pallas as pl
from jax.experimental.pallas import tpu as pltpu
from jax.sharding import PartitionSpec as P

BLK = 3072
SUB = 384
PAIR = 2 * SUB
CHUNK = 256
epsilon = 1e-06


def score_chunk(row_tile, cols, start, width):
    return lax.dot_general(
        row_tile,
        cols[pl.ds(start, width), :],
        (((1,), (1,)), ((), ())),
        preferred_element_type=jnp.float32,
    )


def fold_chunks(best, row_tile, cols, traced=None, masked=None):
    total = cols.shape[0]
    for start in range(0, total, CHUNK):
        width = min(CHUNK, total - start)
        scores = score_chunk(row_tile, cols, start, width)
        if masked is not None and start < SUB:
            row_at = lax.broadcasted_iota(jnp.int32, scores.shape, 0)
            col_at = lax.broadcasted_iota(jnp.int32, scores.shape, 1) + start
            same = (row_at == col_at) & (col_at < SUB) & (masked == 0)
            scores = jnp.where(same, -2.0, scores)
        if traced is not None and start < traced.shape[1]:
            traced[:, pl.ds(start, width)] = jnp.maximum(
                traced[:, pl.ds(start, width)], jnp.max(scores, axis=0, keepdims=True)
            )
        for lane in range(0, width, 128):
            piece = scores[:, lane : lane + 128]
            best = piece if best is None else jnp.maximum(best, piece)
    return best


def over_lanes(best):
    return jnp.max(best.T, axis=0, keepdims=True)


def copies_in(refs, target, sems):
    copies = [
        pltpu.make_async_copy(ref, target.at[pl.ds(block * SUB, SUB)], sems.at[block])
        for block, ref in enumerate(refs)
    ]
    for copy in copies:
        copy.start()
    return copies


def pair_of(rows, index):
    return rows[pl.ds(pl.multiple_of(index * PAIR, PAIR), PAIR), :]


def near_kernel(row_count, col_count, *refs):
    row_refs, col_refs = refs[:row_count], refs[row_count : row_count + col_count]
    lanes_out, rows, cols, row_sems, col_sems = refs[row_count + col_count :]
    col_copies = copies_in(col_refs, cols, col_sems)
    copies_in(row_refs, rows, row_sems)
    for copy in col_copies:
        copy.wait()

    @pl.loop(0, row_count // 2)
    def _(index):
        for part in range(2):
            block = index * 2 + part
            pltpu.make_async_copy(row_refs[0], rows.at[pl.ds(block * SUB, SUB)], row_sems.at[block]).wait()
        lanes_out[index] = fold_chunks(None, pair_of(rows, index), cols, masked=index)


def put_pair(best_out, distance, best):
    tile_col = lax.axis_index("tj")
    chip = lax.rem(tile_col // 2 + distance, lax.axis_size("tj") // 2)
    core = lax.rem(tile_col, 2)
    best_out[chip * 2 + core] = best[:, :SUB]
    best_out[chip * 2 + 1 - core] = best[:, SUB:]


def last_kernel(*refs):
    row_refs, last_refs, first_refs = refs[:8], refs[8:11], refs[11:14]
    lanes, best_out, col_out, rows, last_cols, first_cols, row_sems, col_sems = refs[14:]
    last_copies = copies_in(last_refs, last_cols, col_sems.at[0])
    row_copies = copies_in(row_refs, rows, row_sems)
    first_copies = copies_in(first_refs, first_cols, col_sems.at[1])
    for copy in last_copies:
        copy.wait()
    col_out[...] = jnp.full(col_out.shape, -2.0, jnp.float32)

    @pl.loop(0, 3)
    def _(index):
        for part in range(2):
            block = index * 2 + part
            pltpu.make_async_copy(row_refs[0], rows.at[pl.ds(block * SUB, SUB)], row_sems.at[block]).wait()
        best = fold_chunks(lanes[index], pair_of(rows, index), last_cols, traced=col_out)
        put_pair(best_out, jnp.where(index == 1, 3, index // 2), over_lanes(best))

    for copy in row_copies[6:] + first_copies:
        copy.wait()
    best = fold_chunks(None, pair_of(rows, 3), last_cols, traced=col_out)
    put_pair(best_out, 2, over_lanes(fold_chunks(best, pair_of(rows, 3), first_cols)))


ANYWHERE = pl.BlockSpec(memory_space=pl.ANY)
WHOLE = pl.BlockSpec(memory_space=pltpu.VMEM)


def run_kernel(kernel, out_shape, anywhere, whole, scratch, products):
    width = anywhere[0].shape[1]
    return pl.pallas_call(
        kernel,
        out_shape=out_shape,
        in_specs=[ANYWHERE] * len(anywhere) + [WHOLE] * len(whole),
        out_specs=[WHOLE] * len(out_shape),
        scratch_shapes=scratch,
        cost_estimate=pl.CostEstimate(
            flops=2 * products * SUB * SUB * width, bytes_accessed=products * SUB * width // 2, transcendentals=0
        ),
        compiler_params=pltpu.CompilerParams(vmem_limit_bytes=20 * 2**20),
    )(*anywhere, *whole)


def near_maxima(row_blocks, columns):
    row_count, col_count, width = len(row_blocks), len(columns), columns[0].shape[1]
    return run_kernel(
        functools.partial(near_kernel, row_count, col_count),
        [
            jax.ShapeDtypeStruct((row_count // 2, PAIR, 128), jnp.float32),
        ],
        [*row_blocks, *columns],
        [],
        [
            pltpu.VMEM((row_count * SUB, width), jnp.bfloat16),
            pltpu.VMEM((col_count * SUB, width), jnp.bfloat16),
            pltpu.SemaphoreType.DMA((row_count,)),
            pltpu.SemaphoreType.DMA((col_count,)),
        ],
        row_count * col_count,
    )


def last_maxima(row_blocks, last_columns, first_columns, lanes):
    width = row_blocks[0].shape[1]
    return run_kernel(
        last_kernel,
        [jax.ShapeDtypeStruct((8, 1, SUB), jnp.float32), jax.ShapeDtypeStruct((1, PAIR), jnp.float32)],
        [*row_blocks, *last_columns, *first_columns],
        [lanes],
        [
            pltpu.VMEM((8 * SUB, width), jnp.bfloat16),
            pltpu.VMEM((3 * SUB, width), jnp.bfloat16),
            pltpu.VMEM((3 * SUB, width), jnp.bfloat16),
            pltpu.SemaphoreType.DMA((8,)),
            pltpu.SemaphoreType.DMA((2, 3)),
        ],
        30,
    )


def per_device(corpus, slot_of_row):
    rows_in = corpus[0]
    values = slot_of_row[0]
    src_count, features = rows_in.shape
    lanes = lax.axis_size("tj")
    sub_rows = src_count // 2
    cluster = BLK * lax.axis_size("ti")
    capacity = BLK // (lanes * lanes)
    owners = 2 * lanes
    member = values >= 0
    inside = values % cluster
    owner_of = jnp.where(member, values // cluster * lanes + inside % BLK // sub_rows, owners)
    position = inside % sub_rows
    onehot = owner_of[:, None] == jnp.arange(owners, dtype=jnp.int32)[None, :]
    index = jnp.arange(src_count, dtype=jnp.int32)
    before = (index[None, :] < index[:, None]).astype(jnp.bfloat16)
    ranks = jnp.dot(before, onehot.astype(jnp.bfloat16), preferred_element_type=jnp.float32)
    rank = jnp.sum(jnp.where(onehot, ranks, 0.0), axis=1).astype(jnp.int32)
    slot = jnp.where(member, owner_of * capacity + rank, owners * capacity)
    slots = jnp.arange(owners * capacity, dtype=jnp.int32)[:, None]
    picked = slot[None, :] == slots
    send_places = jnp.sum(jnp.where(picked, position[None, :] + 1, 0), axis=1)
    send_rows = jnp.dot(picked.astype(jnp.bfloat16), rows_in, preferred_element_type=jnp.float32)
    got_places = lax.all_to_all(send_places.reshape(owners, 1, capacity), ("grp", "tj"), 0, 0, tiled=True)
    got_rows = lax.all_to_all(
        send_rows.astype(jnp.bfloat16).reshape(owners, capacity, features), ("grp", "tj"), 0, 0, tiled=True
    ).reshape(owners * capacity, features)
    wanted = jnp.arange(1, sub_rows + 1, dtype=jnp.int32)[:, None]
    place = (got_places.reshape(1, owners * capacity) == wanted).astype(jnp.bfloat16)
    arrived = jnp.dot(place, got_rows, preferred_element_type=jnp.float32)
    row_squares = jnp.sum(arrived * arrived, axis=1, keepdims=True)
    own = (arrived * lax.rsqrt(row_squares + epsilon)).astype(jnp.bfloat16)

    def along_rows(value, pairs):
        return lax.ppermute(value, "ti", pairs)

    def along_cols(value, pairs):
        return lax.ppermute(value, "tj", pairs)

    size = lax.axis_size("ti")
    up = [(i, (i + 2) % size) for i in range(size)]
    down = [(i, (i - 2) % size) for i in range(size)]
    far = [(i, (i + 4) % size) for i in range(size)]
    swap = [(i, i ^ 1) for i in range(size)]
    twin = along_cols(own, swap)
    beside = along_rows(own, swap)
    across = along_rows(own, far)
    low = along_cols(own, up)
    high = along_cols(own, down)

    later, low, high, beside, across = lax.optimization_barrier((own, low, high, beside, across))
    low_twin = along_cols(low, swap)
    high_twin = along_cols(high, swap)
    mid = along_cols(later, far)
    after = along_rows(later, down)
    beside_before = along_rows(beside, up)
    beside_across = along_rows(across, swap)

    near = [own, twin, low, low_twin, high, high_twin]
    (near_lanes,) = near_maxima(near, [own, beside, across])
    mid, near_lanes = lax.optimization_barrier((mid, near_lanes))
    mid_twin = along_cols(mid, swap)
    row_best, col_best = last_maxima(
        [*near, mid, mid_twin], [after, beside_before, beside_across], [own, beside, across], near_lanes
    )
    col_best = col_best.reshape(2, sub_rows)
    parts = lax.all_to_all(row_best, "tj", 0, 0, tiled=True)[:, 0]
    from_before = along_rows(col_best[:1], up)
    from_beside = along_rows(col_best[1:], [(i, ((i ^ 1) - 2) % size) for i in range(size)])
    best = jnp.maximum(jnp.max(parts, axis=0), jnp.maximum(from_before[0], from_beside[0]))
    return best[None, :]


def solution(mesh):
    in_specs = (P("grp", ("ti", "tj"), None), P("grp", ("ti", "tj")))
    out_specs = P("grp", ("ti", "tj"))
    return jax.shard_map(
        per_device, mesh=mesh, in_specs=in_specs, out_specs=out_specs, check_vma=False
    )
```

```python
import functools

import jax
import jax.numpy as jnp
from jax import lax
from jax.experimental import pallas as pl
from jax.experimental.pallas import tpu as pltpu
from jax.sharding import PartitionSpec as P

BLK = 3072
SUB = 384
PAIR = 2 * SUB
CHUNK = 256
epsilon = 1e-06


def score_chunk(row_tile, cols, start, width):
    return lax.dot_general(
        row_tile,
        cols[pl.ds(start, width), :],
        (((1,), (1,)), ((), ())),
        preferred_element_type=jnp.float32,
    )


def fold_chunks(best, row_tile, cols, traced=None, masked=None):
    total = cols.shape[0]
    for start in range(0, total, CHUNK):
        width = min(CHUNK, total - start)
        scores = score_chunk(row_tile, cols, start, width)
        if masked is not None and start < SUB:
            row_at = lax.broadcasted_iota(jnp.int32, scores.shape, 0)
            col_at = lax.broadcasted_iota(jnp.int32, scores.shape, 1) + start
            same = (row_at == col_at) & (col_at < SUB) & (masked == 0)
            scores = jnp.where(same, -2.0, scores)
        if traced is not None and start < traced.shape[1]:
            traced[:, pl.ds(start, width)] = jnp.maximum(
                traced[:, pl.ds(start, width)], jnp.max(scores, axis=0, keepdims=True)
            )
        for lane in range(0, width, 128):
            piece = scores[:, lane : lane + 128]
            best = piece if best is None else jnp.maximum(best, piece)
    return best


def over_lanes(best):
    return jnp.max(best.T, axis=0, keepdims=True)


def copies_in(refs, target, sems):
    copies = [
        pltpu.make_async_copy(ref, target.at[pl.ds(block * SUB, SUB)], sems.at[block])
        for block, ref in enumerate(refs)
    ]
    for copy in copies:
        copy.start()
    return copies


def pair_of(rows, index):
    return rows[pl.ds(pl.multiple_of(index * PAIR, PAIR), PAIR), :]


def near_kernel(row_count, col_count, *refs):
    row_refs, col_refs = refs[:row_count], refs[row_count : row_count + col_count]
    lanes_out, rows, cols, row_sems, col_sems = refs[row_count + col_count :]
    col_copies = copies_in(col_refs, cols, col_sems)
    copies_in(row_refs, rows, row_sems)
    for copy in col_copies:
        copy.wait()

    @pl.loop(0, row_count // 2)
    def _(index):
        for part in range(2):
            block = index * 2 + part
            pltpu.make_async_copy(row_refs[0], rows.at[pl.ds(block * SUB, SUB)], row_sems.at[block]).wait()
        lanes_out[index] = fold_chunks(None, pair_of(rows, index), cols, masked=index)


def put_pair(best_out, distance, best):
    best_out[0, distance] = best[:, :SUB]
    best_out[1, distance] = best[:, SUB:]


def last_kernel(*refs):
    row_refs, last_refs, first_refs = refs[:8], refs[8:11], refs[11:14]
    lanes, best_out, col_out, rows, last_cols, first_cols, row_sems, col_sems = refs[14:]
    last_copies = copies_in(last_refs, last_cols, col_sems.at[0])
    row_copies = copies_in(row_refs, rows, row_sems)
    first_copies = copies_in(first_refs, first_cols, col_sems.at[1])
    for copy in last_copies:
        copy.wait()
    col_out[...] = jnp.full(col_out.shape, -2.0, jnp.float32)

    @pl.loop(0, 3)
    def _(index):
        for part in range(2):
            block = index * 2 + part
            pltpu.make_async_copy(row_refs[0], rows.at[pl.ds(block * SUB, SUB)], row_sems.at[block]).wait()
        best = fold_chunks(lanes[index], pair_of(rows, index), last_cols, traced=col_out)
        put_pair(best_out, jnp.where(index == 1, 3, index // 2), over_lanes(best))

    for copy in row_copies[6:] + first_copies:
        copy.wait()
    best = fold_chunks(None, pair_of(rows, 3), last_cols, traced=col_out)
    put_pair(best_out, 2, over_lanes(fold_chunks(best, pair_of(rows, 3), first_cols)))


ANYWHERE = pl.BlockSpec(memory_space=pl.ANY)
WHOLE = pl.BlockSpec(memory_space=pltpu.VMEM)


def run_kernel(kernel, out_shape, anywhere, whole, scratch, products):
    width = anywhere[0].shape[1]
    return pl.pallas_call(
        kernel,
        out_shape=out_shape,
        in_specs=[ANYWHERE] * len(anywhere) + [WHOLE] * len(whole),
        out_specs=[WHOLE] * len(out_shape),
        scratch_shapes=scratch,
        cost_estimate=pl.CostEstimate(
            flops=2 * products * SUB * SUB * width, bytes_accessed=products * SUB * width // 2, transcendentals=0
        ),
        compiler_params=pltpu.CompilerParams(vmem_limit_bytes=20 * 2**20),
    )(*anywhere, *whole)


def near_maxima(row_blocks, columns):
    row_count, col_count, width = len(row_blocks), len(columns), columns[0].shape[1]
    return run_kernel(
        functools.partial(near_kernel, row_count, col_count),
        [
            jax.ShapeDtypeStruct((row_count // 2, PAIR, 128), jnp.float32),
        ],
        [*row_blocks, *columns],
        [],
        [
            pltpu.VMEM((row_count * SUB, width), jnp.bfloat16),
            pltpu.VMEM((col_count * SUB, width), jnp.bfloat16),
            pltpu.SemaphoreType.DMA((row_count,)),
            pltpu.SemaphoreType.DMA((col_count,)),
        ],
        row_count * col_count,
    )


def last_maxima(row_blocks, last_columns, first_columns, lanes):
    width = row_blocks[0].shape[1]
    return run_kernel(
        last_kernel,
        [jax.ShapeDtypeStruct((2, 4, 1, SUB), jnp.float32), jax.ShapeDtypeStruct((1, PAIR), jnp.float32)],
        [*row_blocks, *last_columns, *first_columns],
        [lanes],
        [
            pltpu.VMEM((8 * SUB, width), jnp.bfloat16),
            pltpu.VMEM((3 * SUB, width), jnp.bfloat16),
            pltpu.VMEM((3 * SUB, width), jnp.bfloat16),
            pltpu.SemaphoreType.DMA((8,)),
            pltpu.SemaphoreType.DMA((2, 3)),
        ],
        30,
    )


def exchange_places(table):
    grp, tile_col = lax.axis_index("grp"), lax.axis_index("tj")
    chip, core = tile_col // 2, tile_col % 2
    lanes = lax.axis_size("tj")
    capacity = table.shape[1]

    def part(value, index):
        return lax.dynamic_index_in_dim(value, index, 0, keepdims=False)

    def in_order(mine, other, index):
        return jnp.where(index == 0, jnp.stack([mine, other]), jnp.stack([other, mine]))

    halves = table.reshape(2, lanes, capacity)
    other = lax.ppermute(part(halves, 1 - grp), "grp", [(0, 1), (1, 0)])
    by_grp = in_order(part(halves, grp), other, grp)
    cores = by_grp.reshape(2, lanes // 2, 2, capacity).transpose(2, 1, 0, 3)
    other = lax.ppermute(part(cores, 1 - core), "tj", [(j, j ^ 1) for j in range(lanes)])
    by_core = in_order(part(cores, core), other, core).transpose(1, 2, 0, 3)
    got = jnp.zeros_like(by_core)
    depth = lanes // 2
    sender = jnp.arange(depth, dtype=jnp.int32)[:, None, None, None]
    for step in range(depth):
        piece = part(by_core, (chip + step) % depth)
        if step:
            piece = lax.ppermute(piece, "tj", [(j, (j + 2 * step) % lanes) for j in range(lanes)])
        got = jnp.where(sender == (chip - step) % depth, piece[None], got)
    return got.transpose(1, 0, 2, 3)


def per_device(corpus, slot_of_row):
    rows_in = corpus[0]
    values = slot_of_row[0]
    src_count, features = rows_in.shape
    lanes = lax.axis_size("tj")
    sub_rows = src_count // 2
    cluster = BLK * lax.axis_size("ti")
    capacity = BLK // (lanes * lanes)
    owners = 2 * lanes
    member = values >= 0
    inside = values % cluster
    owner_of = jnp.where(member, values // cluster * lanes + inside % BLK // sub_rows, owners)
    position = inside % sub_rows
    onehot = owner_of[:, None] == jnp.arange(owners, dtype=jnp.int32)[None, :]
    index = jnp.arange(src_count, dtype=jnp.int32)
    before = (index[None, :] < index[:, None]).astype(jnp.bfloat16)
    ranks = jnp.dot(before, onehot.astype(jnp.bfloat16), preferred_element_type=jnp.float32)
    rank = jnp.sum(jnp.where(onehot, ranks, 0.0), axis=1).astype(jnp.int32)
    slot = jnp.where(member, owner_of * capacity + rank, owners * capacity)
    slots = jnp.arange(owners * capacity, dtype=jnp.int32)[:, None]
    picked = (slot[None, :] == slots).astype(jnp.bfloat16)
    send_rows = jnp.dot(picked, rows_in, preferred_element_type=jnp.float32).astype(jnp.bfloat16)
    got_rows = lax.all_to_all(
        send_rows.reshape(owners, capacity, features), ("grp", "tj"), 0, 0, tiled=True
    ).reshape(owners * capacity, features)

    code = jnp.where(member, position + 1, 0)
    by_rank = (rank[:, None] == jnp.arange(capacity, dtype=jnp.int32)[None, :]).astype(jnp.bfloat16)
    parts = jnp.stack([code // 16 * 16, code % 16]).astype(jnp.bfloat16)
    by_owner = jnp.where(onehot.T[None], parts[:, None, :], 0).reshape(2 * owners, src_count)
    tables = jnp.dot(by_owner, by_rank, preferred_element_type=jnp.float32)
    got_places = exchange_places(tables[:owners] + tables[owners:])
    wanted = jnp.arange(1, sub_rows + 1, dtype=jnp.int32)[:, None]
    place = (got_places.reshape(1, owners * capacity).astype(jnp.int32) == wanted).astype(jnp.bfloat16)
    arrived = jnp.dot(place, got_rows, preferred_element_type=jnp.float32)
    row_squares = jnp.sum(arrived * arrived, axis=1, keepdims=True)
    own = (arrived * lax.rsqrt(row_squares + epsilon)).astype(jnp.bfloat16)

    def along_rows(value, pairs):
        return lax.ppermute(value, "ti", pairs)

    def along_cols(value, pairs):
        return lax.ppermute(value, "tj", pairs)

    size = lax.axis_size("ti")
    up = [(i, (i + 2) % size) for i in range(size)]
    down = [(i, (i - 2) % size) for i in range(size)]
    far = [(i, (i + 4) % size) for i in range(size)]
    swap = [(i, i ^ 1) for i in range(size)]
    twin = along_cols(own, swap)
    beside = along_rows(own, swap)
    across = along_rows(own, far)
    low = along_cols(own, up)
    high = along_cols(own, down)

    later, low, high = lax.optimization_barrier((own, low, high))
    after_own, across = lax.optimization_barrier((own, across))
    low_twin = along_cols(low, swap)
    high_twin = along_cols(high, swap)
    mid = along_cols(later, far)
    after = along_rows(after_own, down)
    beside_before = along_rows(beside, up)
    beside_across = along_rows(across, swap)

    near = [own, twin, low, low_twin, high, high_twin]
    (near_lanes,) = near_maxima(near, [own, beside, across])
    mid, near_lanes = lax.optimization_barrier((mid, near_lanes))
    mid_twin = along_cols(mid, swap)
    row_best, col_best = last_maxima(
        [*near, mid, mid_twin], [after, beside_before, beside_across], [own, beside, across], near_lanes
    )
    col_best = col_best.reshape(2, sub_rows)
    from_before = along_rows(col_best[:1], up)
    from_beside = along_rows(col_best[1:], [(i, ((i ^ 1) - 2) % size) for i in range(size)])
    twin_best = along_cols(row_best[1], swap)
    chip_best = jnp.maximum(row_best[0], twin_best)
    best = jnp.maximum(chip_best[0], jnp.maximum(from_before, from_beside))
    for step in range(1, lanes // 2):
        best = jnp.maximum(best, along_cols(chip_best[step], [(j, (j + 2 * step) % lanes) for j in range(lanes)]))
    return best


def solution(mesh):
    in_specs = (P("grp", ("ti", "tj"), None), P("grp", ("ti", "tj")))
    out_specs = P("grp", ("ti", "tj"))
    return jax.shard_map(
        per_device, mesh=mesh, in_specs=in_specs, out_specs=out_specs, check_vma=False
    )
```

```python
import functools

import jax
import jax.numpy as jnp
from jax import lax
from jax.experimental import pallas as pl
from jax.experimental.pallas import tpu as pltpu
from jax.sharding import PartitionSpec as P

BLK = 3072
SUB = 384
PAIR = 2 * SUB
CHUNK = 256
TAGS = 128
epsilon = 1e-06


def score_chunk(row_tile, cols, start, width):
    return lax.dot_general(
        row_tile,
        cols[pl.ds(start, width), :],
        (((1,), (1,)), ((), ())),
        preferred_element_type=jnp.float32,
    )


def fold_chunks(best, row_tile, cols, traced=None, masked=None):
    total = cols.shape[0]
    for start in range(0, total, CHUNK):
        width = min(CHUNK, total - start)
        scores = score_chunk(row_tile, cols, start, width)
        if masked is not None and start < SUB:
            row_at = lax.broadcasted_iota(jnp.int32, scores.shape, 0)
            col_at = lax.broadcasted_iota(jnp.int32, scores.shape, 1) + start
            same = (row_at == col_at) & (col_at < SUB) & (masked == 0)
            scores = jnp.where(same, -2.0, scores)
        if traced is not None and start < traced.shape[1]:
            traced[:, pl.ds(start, width)] = jnp.maximum(
                traced[:, pl.ds(start, width)], jnp.max(scores, axis=0, keepdims=True)
            )
        for lane in range(0, width, 128):
            piece = scores[:, lane : lane + 128]
            best = piece if best is None else jnp.maximum(best, piece)
    return best


def over_lanes(best):
    return jnp.max(best.T, axis=0, keepdims=True)


def copies_in(refs, target, sems):
    copies = [
        pltpu.make_async_copy(ref, target.at[pl.ds(block * SUB, SUB)], sems.at[block])
        for block, ref in enumerate(refs)
    ]
    for copy in copies:
        copy.start()
    return copies


def pair_of(rows, index):
    return rows[pl.ds(pl.multiple_of(index * PAIR, PAIR), PAIR), :]


def near_kernel(row_count, col_count, *refs):
    row_refs, col_refs = refs[:row_count], refs[row_count : row_count + col_count]
    lanes_out, rows, cols, row_sems, col_sems = refs[row_count + col_count :]
    col_copies = copies_in(col_refs, cols, col_sems)
    copies_in(row_refs, rows, row_sems)
    for copy in col_copies:
        copy.wait()

    @pl.loop(0, row_count // 2)
    def _(index):
        for part in range(2):
            block = index * 2 + part
            pltpu.make_async_copy(row_refs[0], rows.at[pl.ds(block * SUB, SUB)], row_sems.at[block]).wait()
        lanes_out[index] = fold_chunks(None, pair_of(rows, index), cols, masked=index)


def put_pair(best_out, distance, best):
    best_out[0, distance] = best[:, :SUB]
    best_out[1, distance] = best[:, SUB:]


def last_kernel(*refs):
    row_refs, last_refs, first_refs = refs[:8], refs[8:11], refs[11:14]
    lanes, best_out, col_out, rows, last_cols, first_cols, row_sems, col_sems = refs[14:]
    last_copies = copies_in(last_refs, last_cols, col_sems.at[0])
    row_copies = copies_in(row_refs, rows, row_sems)
    first_copies = copies_in(first_refs, first_cols, col_sems.at[1])
    for copy in last_copies:
        copy.wait()
    col_out[...] = jnp.full(col_out.shape, -2.0, jnp.float32)

    @pl.loop(0, 3)
    def _(index):
        for part in range(2):
            block = index * 2 + part
            pltpu.make_async_copy(row_refs[0], rows.at[pl.ds(block * SUB, SUB)], row_sems.at[block]).wait()
        best = fold_chunks(lanes[index], pair_of(rows, index), last_cols, traced=col_out)
        put_pair(best_out, jnp.where(index == 1, 3, index // 2), over_lanes(best))

    for copy in row_copies[6:] + first_copies:
        copy.wait()
    best = fold_chunks(None, pair_of(rows, 3), last_cols, traced=col_out)
    put_pair(best_out, 2, over_lanes(fold_chunks(best, pair_of(rows, 3), first_cols)))


ANYWHERE = pl.BlockSpec(memory_space=pl.ANY)
WHOLE = pl.BlockSpec(memory_space=pltpu.VMEM)


def run_kernel(kernel, out_shape, anywhere, whole, scratch, products):
    width = anywhere[0].shape[1]
    return pl.pallas_call(
        kernel,
        out_shape=out_shape,
        in_specs=[ANYWHERE] * len(anywhere) + [WHOLE] * len(whole),
        out_specs=[WHOLE] * len(out_shape),
        scratch_shapes=scratch,
        cost_estimate=pl.CostEstimate(
            flops=2 * products * SUB * SUB * width, bytes_accessed=products * SUB * width // 2, transcendentals=0
        ),
        compiler_params=pltpu.CompilerParams(vmem_limit_bytes=20 * 2**20),
    )(*anywhere, *whole)


def near_maxima(row_blocks, columns):
    row_count, col_count, width = len(row_blocks), len(columns), columns[0].shape[1]
    return run_kernel(
        functools.partial(near_kernel, row_count, col_count),
        [
            jax.ShapeDtypeStruct((row_count // 2, PAIR, 128), jnp.float32),
        ],
        [*row_blocks, *columns],
        [],
        [
            pltpu.VMEM((row_count * SUB, width), jnp.bfloat16),
            pltpu.VMEM((col_count * SUB, width), jnp.bfloat16),
            pltpu.SemaphoreType.DMA((row_count,)),
            pltpu.SemaphoreType.DMA((col_count,)),
        ],
        row_count * col_count,
    )


def last_maxima(row_blocks, last_columns, first_columns, lanes):
    width = row_blocks[0].shape[1]
    return run_kernel(
        last_kernel,
        [jax.ShapeDtypeStruct((2, 4, 1, SUB), jnp.float32), jax.ShapeDtypeStruct((1, PAIR), jnp.float32)],
        [*row_blocks, *last_columns, *first_columns],
        [lanes],
        [
            pltpu.VMEM((8 * SUB, width), jnp.bfloat16),
            pltpu.VMEM((3 * SUB, width), jnp.bfloat16),
            pltpu.VMEM((3 * SUB, width), jnp.bfloat16),
            pltpu.SemaphoreType.DMA((8,)),
            pltpu.SemaphoreType.DMA((2, 3)),
        ],
        30,
    )


def pack_kernel(capacity, owners, values_ref, rows_ref, send_ref, rows, sem):
    copy = pltpu.make_async_copy(rows_ref, rows, sem)
    copy.start()
    lanes = lax.axis_size("tj")
    cluster = BLK * lax.axis_size("ti")
    count, features = rows.shape
    values = values_ref[...]
    member = values >= 0
    grp = jnp.where(values >= cluster, 1, 0)
    inside = values - grp * cluster - lax.axis_index("ti") * BLK
    part = jnp.zeros_like(inside)
    for step in range(1, lanes):
        part = part + jnp.where(inside >= step * SUB, 1, 0)
    code = inside - part * SUB + 1
    owner = jnp.where(member, grp * lanes + part, -1)
    owned = lax.broadcasted_iota(jnp.int32, (owners, count), 0) == owner
    index = lax.broadcasted_iota(jnp.int32, (count, count), 0)
    before = jnp.where(index < lax.broadcasted_iota(jnp.int32, (count, count), 1), 1.0, 0.0).astype(jnp.bfloat16)
    ranks = jnp.dot(jnp.where(owned, 1.0, 0.0).astype(jnp.bfloat16), before, preferred_element_type=jnp.float32)
    rank = jnp.sum(jnp.where(owned, ranks, 0.0), axis=0, keepdims=True).astype(jnp.int32)
    slot = jnp.where(member, owner * capacity + rank, -1)
    tag_at = lax.broadcasted_iota(jnp.int32, (TAGS, count), 0)
    low_part = code & 15
    tags = jnp.where(tag_at == 0, code - low_part, jnp.where(tag_at == 1, low_part, 0))
    tags = tags.astype(jnp.float32).astype(jnp.bfloat16)
    copy.wait()
    for start in range(0, owners * capacity, CHUNK):
        at = lax.broadcasted_iota(jnp.int32, (CHUNK, count), 0) + start
        picked = jnp.where(at == slot, 1.0, 0.0).astype(jnp.bfloat16)
        taken = jnp.dot(picked, rows[...], preferred_element_type=jnp.float32)
        send_ref[pl.ds(start, CHUNK), :features] = taken.astype(jnp.bfloat16)
        places = lax.dot_general(picked, tags, (((1,), (1,)), ((), ())), preferred_element_type=jnp.float32)
        send_ref[pl.ds(start, CHUNK), features:] = places.astype(jnp.bfloat16)


def pack_rows(values, rows, capacity, owners):
    count, features = rows.shape
    return pl.pallas_call(
        functools.partial(pack_kernel, capacity, owners),
        out_shape=jax.ShapeDtypeStruct((owners * capacity, features + TAGS), jnp.bfloat16),
        in_specs=[WHOLE, ANYWHERE],
        out_specs=WHOLE,
        scratch_shapes=[pltpu.VMEM((count, features), jnp.bfloat16), pltpu.SemaphoreType.DMA],
        cost_estimate=pl.CostEstimate(
            flops=2 * owners * capacity * count * features, bytes_accessed=4 * count * features, transcendentals=0
        ),
        compiler_params=pltpu.CompilerParams(vmem_limit_bytes=20 * 2**20),
    )(values, rows)


def per_device(corpus, slot_of_row):
    rows_in = corpus[0]
    values = slot_of_row[0]
    src_count, features = rows_in.shape
    lanes = lax.axis_size("tj")
    sub_rows = src_count // 2
    capacity = BLK // (lanes * lanes)
    owners = 2 * lanes
    send = pack_rows(values[None, :], rows_in, capacity, owners).reshape(owners, capacity, features + TAGS)
    got = lax.all_to_all(send, ("grp", "tj"), 0, 0, tiled=True).reshape(owners * capacity, features + TAGS)
    sum_tags = jnp.where(jnp.arange(TAGS, dtype=jnp.int32)[None, :] < 2, 1.0, 0.0).astype(jnp.bfloat16)
    got_places = lax.dot_general(
        sum_tags, got[:, features:], (((1,), (1,)), ((), ())), preferred_element_type=jnp.float32
    )
    wanted = jnp.arange(1, sub_rows + 1, dtype=jnp.int32)[:, None]
    place = (got_places.astype(jnp.int32) == wanted).astype(jnp.bfloat16)
    arrived = jnp.dot(place, got[:, :features], preferred_element_type=jnp.float32)
    row_squares = jnp.sum(arrived * arrived, axis=1, keepdims=True)
    own = (arrived * lax.rsqrt(row_squares + epsilon)).astype(jnp.bfloat16)

    def along_rows(value, pairs):
        return lax.ppermute(value, "ti", pairs)

    def along_cols(value, pairs):
        return lax.ppermute(value, "tj", pairs)

    size = lax.axis_size("ti")
    up = [(i, (i + 2) % size) for i in range(size)]
    down = [(i, (i - 2) % size) for i in range(size)]
    far = [(i, (i + 4) % size) for i in range(size)]
    swap = [(i, i ^ 1) for i in range(size)]
    twin = along_cols(own, swap)
    beside = along_rows(own, swap)
    across = along_rows(own, far)
    low = along_cols(own, up)
    high = along_cols(own, down)

    later, low, high = lax.optimization_barrier((own, low, high))
    after_own, across = lax.optimization_barrier((own, across))
    low_twin = along_cols(low, swap)
    high_twin = along_cols(high, swap)
    mid = along_cols(later, far)
    after = along_rows(after_own, down)
    beside_before = along_rows(beside, up)
    beside_across = along_rows(across, swap)

    near = [own, twin, low, low_twin, high, high_twin]
    (near_lanes,) = near_maxima(near, [own, beside, across])
    mid, near_lanes = lax.optimization_barrier((mid, near_lanes))
    mid_twin = along_cols(mid, swap)
    row_best, col_best = last_maxima(
        [*near, mid, mid_twin], [after, beside_before, beside_across], [own, beside, across], near_lanes
    )
    col_best = col_best.reshape(2, sub_rows)
    from_before = along_rows(col_best[:1], up)
    from_beside = along_rows(col_best[1:], [(i, ((i ^ 1) - 2) % size) for i in range(size)])
    twin_best = along_cols(row_best[1], swap)
    chip_best = jnp.maximum(row_best[0], twin_best)
    best = jnp.maximum(chip_best[0], jnp.maximum(from_before, from_beside))
    for step in range(1, lanes // 2):
        best = jnp.maximum(best, along_cols(chip_best[step], [(j, (j + 2 * step) % lanes) for j in range(lanes)]))
    return best


def solution(mesh):
    in_specs = (P("grp", ("ti", "tj"), None), P("grp", ("ti", "tj")))
    out_specs = P("grp", ("ti", "tj"))
    return jax.shard_map(
        per_device, mesh=mesh, in_specs=in_specs, out_specs=out_specs, check_vma=False
    )
```

```python
import functools

import jax
import jax.numpy as jnp
from jax import lax
from jax.experimental import pallas as pl
from jax.experimental.pallas import tpu as pltpu
from jax.sharding import PartitionSpec as P

BLK = 3072
SUB = 384
PAIR = 2 * SUB
CHUNK = 256
TAGS = 128
epsilon = 1e-06


def score_chunk(row_tile, cols, start, width):
    return lax.dot_general(
        row_tile,
        cols[pl.ds(start, width), :],
        (((1,), (1,)), ((), ())),
        preferred_element_type=jnp.float32,
    )


def fold_chunks(best, row_tile, cols, traced=None, masked=None):
    total = cols.shape[0]
    for start in range(0, total, CHUNK):
        width = min(CHUNK, total - start)
        scores = score_chunk(row_tile, cols, start, width)
        if masked is not None and start < SUB:
            row_at = lax.broadcasted_iota(jnp.int32, scores.shape, 0)
            col_at = lax.broadcasted_iota(jnp.int32, scores.shape, 1) + start
            same = (row_at == col_at) & (col_at < SUB) & (masked == 0)
            scores = jnp.where(same, -2.0, scores)
        if traced is not None and start < traced.shape[1]:
            traced[:, pl.ds(start, width)] = jnp.maximum(
                traced[:, pl.ds(start, width)], jnp.max(scores, axis=0, keepdims=True)
            )
        for lane in range(0, width, 128):
            piece = scores[:, lane : lane + 128]
            best = piece if best is None else jnp.maximum(best, piece)
    return best


def over_lanes(best):
    return jnp.max(best.T, axis=0, keepdims=True)


def copies_in(refs, target, sems):
    height = refs[0].shape[0]
    copies = [
        pltpu.make_async_copy(ref, target.at[pl.ds(block * height, height)], sems.at[block])
        for block, ref in enumerate(refs)
    ]
    for copy in copies:
        copy.start()
    return copies


def pair_of(rows, index):
    return rows[pl.ds(pl.multiple_of(index * PAIR, PAIR), PAIR), :]


def near_kernel(row_count, col_count, *refs):
    row_refs, col_refs = refs[:row_count], refs[row_count : row_count + col_count]
    lanes_out, rows, cols, row_sems, col_sems = refs[row_count + col_count :]
    col_copies = copies_in(col_refs, cols, col_sems)
    copies_in(row_refs, rows, row_sems)
    for copy in col_copies:
        copy.wait()

    @pl.loop(0, row_count // 2)
    def _(index):
        for part in range(2):
            block = index * 2 + part
            pltpu.make_async_copy(row_refs[0], rows.at[pl.ds(block * SUB, SUB)], row_sems.at[block]).wait()
        lanes_out[index] = fold_chunks(None, pair_of(rows, index), cols, masked=index)


def mid_kernel(row_count, col_count, *refs):
    row_refs, col_refs = refs[:row_count], refs[row_count : row_count + col_count]
    lanes_out, rows, cols, row_sems, col_sems = refs[row_count + col_count :]
    for copy in copies_in(col_refs, cols, col_sems) + copies_in(row_refs, rows, row_sems):
        copy.wait()
    lanes_out[0] = fold_chunks(None, rows[...], cols)


def put_pair(best_out, distance, best):
    best_out[0, distance] = best[:, :SUB]
    best_out[1, distance] = best[:, SUB:]


def last_kernel(*refs):
    near_refs, mid_refs, last_refs = refs[:6], refs[6:10], refs[10:13]
    near_lanes, mid_lanes, best_out, col_out, rows, last_cols, row_sems, mid_sems, col_sems = refs[13:]
    last_copies = copies_in(last_refs, last_cols, col_sems)
    copies_in(near_refs, rows, row_sems)
    mid_copies = copies_in(mid_refs, rows.at[pl.ds(3 * PAIR, PAIR)], mid_sems)
    for copy in last_copies:
        copy.wait()
    col_out[...] = jnp.full(col_out.shape, -2.0, jnp.float32)

    @pl.loop(0, 3)
    def _(index):
        for part in range(2):
            block = index * 2 + part
            pltpu.make_async_copy(near_refs[0], rows.at[pl.ds(block * SUB, SUB)], row_sems.at[block]).wait()
        best = fold_chunks(near_lanes[index], pair_of(rows, index), last_cols, traced=col_out)
        put_pair(best_out, jnp.where(index == 1, 3, index // 2), over_lanes(best))

    for copy in mid_copies:
        copy.wait()
    put_pair(best_out, 2, over_lanes(fold_chunks(mid_lanes[0], pair_of(rows, 3), last_cols, traced=col_out)))


ANYWHERE = pl.BlockSpec(memory_space=pl.ANY)
WHOLE = pl.BlockSpec(memory_space=pltpu.VMEM)


def run_kernel(kernel, out_shape, anywhere, whole, scratch, products):
    width = anywhere[0].shape[1]
    return pl.pallas_call(
        kernel,
        out_shape=out_shape,
        in_specs=[ANYWHERE] * len(anywhere) + [WHOLE] * len(whole),
        out_specs=[WHOLE] * len(out_shape),
        scratch_shapes=scratch,
        cost_estimate=pl.CostEstimate(
            flops=2 * products * SUB * SUB * width, bytes_accessed=products * SUB * width // 2, transcendentals=0
        ),
        compiler_params=pltpu.CompilerParams(vmem_limit_bytes=20 * 2**20),
    )(*anywhere, *whole)


def first_maxima(kernel, row_blocks, columns):
    row_count, col_count, width = len(row_blocks), len(columns), columns[0].shape[1]
    total = row_count * row_blocks[0].shape[0]
    return run_kernel(
        functools.partial(kernel, row_count, col_count),
        [jax.ShapeDtypeStruct((total // PAIR, PAIR, 128), jnp.float32)],
        [*row_blocks, *columns],
        [],
        [
            pltpu.VMEM((total, width), jnp.bfloat16),
            pltpu.VMEM((col_count * SUB, width), jnp.bfloat16),
            pltpu.SemaphoreType.DMA((row_count,)),
            pltpu.SemaphoreType.DMA((col_count,)),
        ],
        total // SUB * col_count,
    )


def last_maxima(row_blocks, last_columns, near_lanes, mid_lanes):
    width = row_blocks[0].shape[1]
    return run_kernel(
        last_kernel,
        [jax.ShapeDtypeStruct((2, 4, 1, SUB), jnp.float32), jax.ShapeDtypeStruct((1, PAIR), jnp.float32)],
        [*row_blocks, *last_columns],
        [near_lanes, mid_lanes],
        [
            pltpu.VMEM((8 * SUB, width), jnp.bfloat16),
            pltpu.VMEM((3 * SUB, width), jnp.bfloat16),
            pltpu.SemaphoreType.DMA((6,)),
            pltpu.SemaphoreType.DMA((4,)),
            pltpu.SemaphoreType.DMA((3,)),
        ],
        24,
    )


def pack_kernel(capacity, owners, values_ref, rows_ref, send_ref, rows, sem):
    copy = pltpu.make_async_copy(rows_ref, rows, sem)
    copy.start()
    lanes = lax.axis_size("tj")
    cluster = BLK * lax.axis_size("ti")
    count, features = rows.shape
    values = values_ref[...]
    member = values >= 0
    grp = jnp.where(values >= cluster, 1, 0)
    inside = values - grp * cluster - lax.axis_index("ti") * BLK
    part = jnp.zeros_like(inside)
    for step in range(1, lanes):
        part = part + jnp.where(inside >= step * SUB, 1, 0)
    code = inside - part * SUB + 1
    owner = jnp.where(member, grp * lanes + part, -1)
    owned = lax.broadcasted_iota(jnp.int32, (owners, count), 0) == owner
    index = lax.broadcasted_iota(jnp.int32, (count, count), 0)
    before = jnp.where(index < lax.broadcasted_iota(jnp.int32, (count, count), 1), 1.0, 0.0).astype(jnp.bfloat16)
    ranks = jnp.dot(jnp.where(owned, 1.0, 0.0).astype(jnp.bfloat16), before, preferred_element_type=jnp.float32)
    rank = jnp.sum(jnp.where(owned, ranks, 0.0), axis=0, keepdims=True).astype(jnp.int32)
    slot = jnp.where(member, owner * capacity + rank, -1)
    tag_at = lax.broadcasted_iota(jnp.int32, (TAGS, count), 0)
    low_part = code & 15
    tags = jnp.where(tag_at == 0, code - low_part, jnp.where(tag_at == 1, low_part, 0))
    tags = tags.astype(jnp.float32).astype(jnp.bfloat16)
    copy.wait()
    for start in range(0, owners * capacity, CHUNK):
        at = lax.broadcasted_iota(jnp.int32, (CHUNK, count), 0) + start
        picked = jnp.where(at == slot, 1.0, 0.0).astype(jnp.bfloat16)
        taken = jnp.dot(picked, rows[...], preferred_element_type=jnp.float32)
        send_ref[pl.ds(start, CHUNK), :features] = taken.astype(jnp.bfloat16)
        places = lax.dot_general(picked, tags, (((1,), (1,)), ((), ())), preferred_element_type=jnp.float32)
        send_ref[pl.ds(start, CHUNK), features:] = places.astype(jnp.bfloat16)


def pack_rows(values, rows, capacity, owners):
    count, features = rows.shape
    return pl.pallas_call(
        functools.partial(pack_kernel, capacity, owners),
        out_shape=jax.ShapeDtypeStruct((owners * capacity, features + TAGS), jnp.bfloat16),
        in_specs=[WHOLE, ANYWHERE],
        out_specs=WHOLE,
        scratch_shapes=[pltpu.VMEM((count, features), jnp.bfloat16), pltpu.SemaphoreType.DMA],
        cost_estimate=pl.CostEstimate(
            flops=2 * owners * capacity * count * features, bytes_accessed=4 * count * features, transcendentals=0
        ),
        compiler_params=pltpu.CompilerParams(vmem_limit_bytes=56 * 2**20),
    )(values, rows)


def per_device(corpus, slot_of_row):
    rows_in = corpus[0]
    src_count, features = rows_in.shape
    lanes = lax.axis_size("tj")
    sub_rows = src_count // 2
    capacity = BLK // (lanes * lanes)
    owners = 2 * lanes
    send = pack_rows(slot_of_row, rows_in, capacity, owners).reshape(owners, capacity, features + TAGS)
    got = lax.all_to_all(send, ("grp", "tj"), 0, 0, tiled=True).reshape(owners * capacity, features + TAGS)
    sum_tags = jnp.where(jnp.arange(TAGS, dtype=jnp.int32)[None, :] < 2, 1.0, 0.0).astype(jnp.bfloat16)
    got_places = lax.dot_general(
        sum_tags, got[:, features:], (((1,), (1,)), ((), ())), preferred_element_type=jnp.float32
    )
    wanted = jnp.arange(1, sub_rows + 1, dtype=jnp.int32)[:, None]
    place = (got_places.astype(jnp.int32) == wanted).astype(jnp.bfloat16)
    arrived = jnp.dot(place, got[:, :features], preferred_element_type=jnp.float32)
    row_squares = jnp.sum(arrived * arrived, axis=1, keepdims=True)
    own = (arrived * lax.rsqrt(row_squares + epsilon)).astype(jnp.bfloat16)

    def along_rows(value, pairs):
        return lax.ppermute(value, "ti", pairs)

    def along_cols(value, pairs):
        return lax.ppermute(value, "tj", pairs)

    size = lax.axis_size("ti")
    up = [(i, (i + 2) % size) for i in range(size)]
    down = [(i, (i - 2) % size) for i in range(size)]
    far = [(i, (i + 4) % size) for i in range(size)]
    swap = [(i, i ^ 1) for i in range(size)]
    twin = along_cols(own, swap)
    beside = along_rows(own, swap)
    across = along_rows(own, far)
    low = along_cols(own, up)
    high = along_cols(own, down)

    later, across = lax.optimization_barrier((own, across))
    low_twin = along_cols(low, swap)
    high_twin = along_cols(high, swap)
    half = sub_rows // 2
    mid_top = along_cols(low[:half], up)
    mid_bottom = along_cols(high[half:], down)
    after = along_rows(later, down)
    beside_before = along_rows(beside, up)
    beside_across = along_rows(across, swap)

    near = [own, twin, low, low_twin, high, high_twin]
    (near_lanes,) = first_maxima(near_kernel, near, [own, beside, across])
    mid_top, mid_bottom, near_lanes = lax.optimization_barrier((mid_top, mid_bottom, near_lanes))
    mid = [mid_top, mid_bottom, along_cols(mid_top, swap), along_cols(mid_bottom, swap)]
    (mid_lanes,) = first_maxima(mid_kernel, mid, [own, beside, across])
    row_best, col_best = last_maxima(
        [*near, *mid], [after, beside_before, beside_across], near_lanes, mid_lanes
    )
    col_best = col_best.reshape(2, sub_rows)
    from_before = along_rows(col_best[:1], up)
    from_beside = along_rows(col_best[1:], [(i, ((i ^ 1) - 2) % size) for i in range(size)])
    twin_best = along_cols(row_best[1], swap)
    chip_best = jnp.maximum(row_best[0], twin_best)
    best = jnp.maximum(chip_best[0], jnp.maximum(from_before, from_beside))
    for step in range(1, lanes // 2):
        best = jnp.maximum(best, along_cols(chip_best[step], [(j, (j + 2 * step) % lanes) for j in range(lanes)]))
    return best


def solution(mesh):
    in_specs = (P("grp", ("ti", "tj"), None), P("grp", ("ti", "tj")))
    out_specs = P("grp", ("ti", "tj"))
    return jax.shard_map(
        per_device, mesh=mesh, in_specs=in_specs, out_specs=out_specs, check_vma=False
    )
```

```python
import functools

import jax
import jax.numpy as jnp
from jax import lax
from jax.experimental import pallas as pl
from jax.experimental.pallas import tpu as pltpu
from jax.sharding import PartitionSpec as P

BLK = 3072
SUB = 384
PAIR = 2 * SUB
CHUNK = 256
NEAR = 6
TAGS = 128
epsilon = 1e-06


def score_chunk(row_tile, cols, start, width):
    return lax.dot_general(
        row_tile,
        cols[pl.ds(start, width), :],
        (((1,), (1,)), ((), ())),
        preferred_element_type=jnp.float32,
    )


def fold_chunks(best, row_tile, cols, traced=None, first_tile=None, before=None):
    total = cols.shape[0]
    for start in range(0, total, CHUNK):
        width = min(CHUNK, total - start)
        if before is not None:
            before(start + width)
        scores = score_chunk(row_tile, cols, start, width)
        if first_tile is not None and start < SUB:
            row_at = lax.broadcasted_iota(jnp.int32, scores.shape, 0)
            col_at = lax.broadcasted_iota(jnp.int32, scores.shape, 1) + start
            same = (row_at == col_at) & (col_at < SUB) & first_tile
            scores = jnp.where(same, -2.0, scores)
        if traced is not None and start < traced.shape[1]:
            traced[:, pl.ds(start, width)] = jnp.maximum(
                traced[:, pl.ds(start, width)], jnp.max(scores, axis=0, keepdims=True)
            )
        for lane in range(0, width, 128):
            piece = scores[:, lane : lane + 128]
            best = piece if best is None else jnp.maximum(best, piece)
    return best


def over_lanes(best):
    return jnp.max(best.T, axis=0, keepdims=True)


def copies_in(refs, target, sems):
    height = refs[0].shape[0]
    copies = [
        pltpu.make_async_copy(ref, target.at[pl.ds(block * height, height)], sems.at[block])
        for block, ref in enumerate(refs)
    ]
    for copy in copies:
        copy.start()
    return copies


def tile_of(array, index, size):
    return array[pl.ds(pl.multiple_of(index * size, size), size), :]


def near_kernel(*refs):
    row_refs, col_refs = refs[:NEAR], refs[NEAR : NEAR + 3]
    lanes_out, rows, cols, row_sems, col_sems = refs[NEAR + 3 :]
    col_copies = copies_in(col_refs, cols, col_sems)
    copies_in(row_refs, rows, row_sems)
    for copy in col_copies:
        copy.wait()
    blocks = 3

    @pl.loop(0, NEAR // blocks)
    def _(index):
        for part in range(blocks):
            block = index * blocks + part
            pltpu.make_async_copy(row_refs[0], rows.at[pl.ds(block * SUB, SUB)], row_sems.at[block]).wait()
        size = blocks * SUB
        best = fold_chunks(None, tile_of(rows, index, size), cols, first_tile=index == 0)
        lanes_out[pl.ds(pl.multiple_of(index * size, size), size), :] = best


def mid_kernel(*refs):
    row_refs, col_refs = refs[:4], refs[4:7]
    _, _, lanes_out, rows_out, lanes, rows, cols, row_sems, col_sems, out_sems = refs[7:]
    for copy in copies_in(col_refs, cols, col_sems) + copies_in(row_refs, rows, row_sems):
        copy.wait()
    at = pl.ds(NEAR * SUB, PAIR)
    rows_copy = pltpu.make_async_copy(rows, rows_out.at[at], out_sems.at[0])
    rows_copy.start()
    lanes[...] = fold_chunks(None, rows[...], cols)
    lanes_copy = pltpu.make_async_copy(lanes, lanes_out.at[at], out_sems.at[1])
    lanes_copy.start()
    rows_copy.wait()
    lanes_copy.wait()


def last_kernel(after_ref, beside_before_ref, beside_across_ref, lanes, rows, best_out, col_out, cols, sems):
    copies = copies_in((after_ref, beside_before_ref, beside_across_ref), cols, sems)
    col_out[...] = jnp.full(col_out.shape, -2.0, jnp.float32)
    size = 2 * PAIR

    @pl.loop(0, rows.shape[0] // size)
    def _(index):
        waiting = list(enumerate(copies))

        def before(needed):
            while waiting and waiting[0][0] * SUB < needed:
                copy = waiting.pop(0)[1]
                pl.when(index == 0)(copy.wait)

        lanes_tile = lanes[pl.ds(pl.multiple_of(index * size, size), size), :]
        best = fold_chunks(lanes_tile, tile_of(rows, index, size), cols, traced=col_out, before=before)
        best = over_lanes(best)
        for half in range(2):
            order = index * 2 + half
            distance = jnp.where(order == 1, 3, jnp.where(order == 2, 1, jnp.where(order == 3, 2, 0)))
            for core in range(2):
                begin = half * PAIR + core * SUB
                best_out[core, distance] = best[:, begin : begin + SUB]


ANYWHERE = pl.BlockSpec(memory_space=pl.ANY)
WHOLE = pl.BlockSpec(memory_space=pltpu.VMEM)


def run_kernel(kernel, out_shape, anywhere, whole, scratch, products, aliases=None):
    width = anywhere[0].shape[1]
    return pl.pallas_call(
        kernel,
        out_shape=out_shape,
        in_specs=[ANYWHERE] * len(anywhere) + [WHOLE] * len(whole),
        out_specs=[ANYWHERE if aliases else WHOLE] * len(out_shape),
        scratch_shapes=scratch,
        input_output_aliases=aliases or {},
        cost_estimate=pl.CostEstimate(
            flops=2 * products * SUB * SUB * width, bytes_accessed=products * SUB * width // 2, transcendentals=0
        ),
        compiler_params=pltpu.CompilerParams(vmem_limit_bytes=20 * 2**20),
    )(*anywhere, *whole)


def near_maxima(row_blocks, columns):
    width = columns[0].shape[1]
    total = len(row_blocks) * SUB + PAIR
    return run_kernel(
        near_kernel,
        [jax.ShapeDtypeStruct((total, 128), jnp.float32), jax.ShapeDtypeStruct((total, width), jnp.bfloat16)],
        [*row_blocks, *columns],
        [],
        [
            pltpu.VMEM((len(columns) * SUB, width), jnp.bfloat16),
            pltpu.SemaphoreType.DMA((len(row_blocks),)),
            pltpu.SemaphoreType.DMA((len(columns),)),
        ],
        len(row_blocks) * len(columns),
    )


def mid_maxima(row_blocks, columns, lanes, rows):
    width = columns[0].shape[1]
    count = len(row_blocks) + len(columns)
    return run_kernel(
        mid_kernel,
        [jax.ShapeDtypeStruct(lanes.shape, lanes.dtype), jax.ShapeDtypeStruct(rows.shape, rows.dtype)],
        [*row_blocks, *columns, lanes, rows],
        [],
        [
            pltpu.VMEM((PAIR, 128), jnp.float32),
            pltpu.VMEM((PAIR, width), jnp.bfloat16),
            pltpu.VMEM((len(columns) * SUB, width), jnp.bfloat16),
            pltpu.SemaphoreType.DMA((len(row_blocks),)),
            pltpu.SemaphoreType.DMA((len(columns),)),
            pltpu.SemaphoreType.DMA((2,)),
        ],
        2 * len(columns),
        {count: 0, count + 1: 1},
    )


def last_maxima(columns, lanes, rows):
    return run_kernel(
        last_kernel,
        [jax.ShapeDtypeStruct((2, 4, 1, SUB), jnp.float32), jax.ShapeDtypeStruct((1, PAIR), jnp.float32)],
        columns,
        [lanes, rows],
        [pltpu.VMEM((len(columns) * SUB, rows.shape[1]), jnp.bfloat16), pltpu.SemaphoreType.DMA((len(columns),))],
        24,
    )


def pack_kernel(capacity, owners, values_ref, rows_ref, send_ref, rows, sem):
    copy = pltpu.make_async_copy(rows_ref, rows, sem)
    copy.start()
    lanes = lax.axis_size("tj")
    cluster = BLK * lax.axis_size("ti")
    count, features = rows.shape
    values = values_ref[...]
    member = values >= 0
    grp = jnp.where(values >= cluster, 1, 0)
    inside = values - grp * cluster - lax.axis_index("ti") * BLK
    part = jnp.zeros_like(inside)
    for step in range(1, lanes):
        part = part + jnp.where(inside >= step * SUB, 1, 0)
    code = inside - part * SUB + 1
    owner = jnp.where(member, grp * lanes + part, -1)
    owned = lax.broadcasted_iota(jnp.int32, (owners, count), 0) == owner
    index = lax.broadcasted_iota(jnp.int32, (count, count), 0)
    before = jnp.where(index < lax.broadcasted_iota(jnp.int32, (count, count), 1), 1.0, 0.0).astype(jnp.bfloat16)
    ranks = jnp.dot(jnp.where(owned, 1.0, 0.0).astype(jnp.bfloat16), before, preferred_element_type=jnp.float32)
    rank = jnp.sum(jnp.where(owned, ranks, 0.0), axis=0, keepdims=True).astype(jnp.int32)
    slot = jnp.where(member, owner * capacity + rank, -1)
    tag_at = lax.broadcasted_iota(jnp.int32, (TAGS, count), 0)
    low_part = code & 15
    tags = jnp.where(tag_at == 0, code - low_part, jnp.where(tag_at == 1, low_part, 0))
    tags = tags.astype(jnp.float32).astype(jnp.bfloat16)
    copy.wait()

    @pl.loop(0, owners * capacity // CHUNK)
    def _(step):
        start = pl.multiple_of(step * CHUNK, CHUNK)
        at = lax.broadcasted_iota(jnp.int32, (CHUNK, count), 0) + start
        picked = jnp.where(at == slot, 1.0, 0.0).astype(jnp.bfloat16)
        taken = jnp.dot(picked, rows[...], preferred_element_type=jnp.float32)
        send_ref[pl.ds(start, CHUNK), :features] = taken.astype(jnp.bfloat16)
        places = lax.dot_general(picked, tags, (((1,), (1,)), ((), ())), preferred_element_type=jnp.float32)
        send_ref[pl.ds(start, CHUNK), features:] = places.astype(jnp.bfloat16)


def pack_rows(values, rows, capacity, owners):
    count, features = rows.shape
    return pl.pallas_call(
        functools.partial(pack_kernel, capacity, owners),
        out_shape=jax.ShapeDtypeStruct((owners * capacity, features + TAGS), jnp.bfloat16),
        in_specs=[WHOLE, ANYWHERE],
        out_specs=WHOLE,
        scratch_shapes=[pltpu.VMEM((count, features), jnp.bfloat16), pltpu.SemaphoreType.DMA],
        cost_estimate=pl.CostEstimate(
            flops=2 * owners * capacity * count * features, bytes_accessed=4 * count * features, transcendentals=0
        ),
        compiler_params=pltpu.CompilerParams(vmem_limit_bytes=56 * 2**20),
    )(values, rows)


def per_device(corpus, slot_of_row):
    rows_in = corpus[0]
    src_count, features = rows_in.shape
    lanes = lax.axis_size("tj")
    sub_rows = src_count // 2
    capacity = BLK // (lanes * lanes)
    owners = 2 * lanes
    send = pack_rows(slot_of_row, rows_in, capacity, owners).reshape(owners, capacity, features + TAGS)
    got = lax.all_to_all(send, ("grp", "tj"), 0, 0, tiled=True).reshape(owners * capacity, features + TAGS)
    sum_tags = jnp.where(jnp.arange(TAGS, dtype=jnp.int32)[None, :] < 2, 1.0, 0.0).astype(jnp.bfloat16)
    got_places = lax.dot_general(
        sum_tags, got[:, features:], (((1,), (1,)), ((), ())), preferred_element_type=jnp.float32
    )
    wanted = jnp.arange(1, sub_rows + 1, dtype=jnp.int32)[:, None]
    place = (got_places.astype(jnp.int32) == wanted).astype(jnp.bfloat16)
    arrived = jnp.dot(place, got[:, :features], preferred_element_type=jnp.float32)
    row_squares = jnp.sum(arrived * arrived, axis=1, keepdims=True)
    own = (arrived * lax.rsqrt(row_squares + epsilon)).astype(jnp.bfloat16)

    def along_rows(value, pairs):
        return lax.ppermute(value, "ti", pairs)

    def along_cols(value, pairs):
        return lax.ppermute(value, "tj", pairs)

    size = lax.axis_size("ti")
    up = [(i, (i + 2) % size) for i in range(size)]
    down = [(i, (i - 2) % size) for i in range(size)]
    far = [(i, (i + 4) % size) for i in range(size)]
    swap = [(i, i ^ 1) for i in range(size)]
    twin = along_cols(own, swap)
    beside = along_rows(own, swap)
    across = along_rows(own, far)
    low = along_cols(own, up)
    high = along_cols(own, down)

    later, across = lax.optimization_barrier((own, across))
    low_twin = along_cols(low, swap)
    high_twin = along_cols(high, swap)
    half = sub_rows // 2
    mid_top = along_cols(low[:half], up)
    mid_bottom = along_cols(high[half:], down)
    after = along_rows(later, down)
    beside_before = along_rows(beside, up)
    beside_across = along_rows(across, swap)

    lanes_best, rows = near_maxima([own, twin, low, low_twin, high, high_twin], [own, beside, across])
    mid_top, mid_bottom, lanes_best = lax.optimization_barrier((mid_top, mid_bottom, lanes_best))
    mid = [mid_top, mid_bottom, along_cols(mid_top, swap), along_cols(mid_bottom, swap)]
    lanes_best, rows = mid_maxima(mid, [own, beside, across], lanes_best, rows)
    row_best, col_best = last_maxima([after, beside_before, beside_across], lanes_best, rows)
    col_best = col_best.reshape(2, sub_rows)
    from_before = along_rows(col_best[:1], up)
    from_beside = along_rows(col_best[1:], [(i, ((i ^ 1) - 2) % size) for i in range(size)])
    twin_best = along_cols(row_best[1], swap)
    chip_best = jnp.maximum(row_best[0], twin_best)
    best = jnp.maximum(chip_best[0], jnp.maximum(from_before, from_beside))
    for step in range(1, lanes // 2):
        best = jnp.maximum(best, along_cols(chip_best[step], [(j, (j + 2 * step) % lanes) for j in range(lanes)]))
    return best


def solution(mesh):
    in_specs = (P("grp", ("ti", "tj"), None), P("grp", ("ti", "tj")))
    out_specs = P("grp", ("ti", "tj"))
    return jax.shard_map(
        per_device, mesh=mesh, in_specs=in_specs, out_specs=out_specs, check_vma=False
    )
```

```python
import functools

import jax
import jax.numpy as jnp
from jax import lax
from jax.experimental import pallas as pl
from jax.experimental.pallas import tpu as pltpu
from jax.sharding import PartitionSpec as P

BLK = 3072
SUB = 384
PAIR = 2 * SUB
CHUNK = 256
NEAR = 6
EARLY = 1024
TAGS = 128
BLOCK = 128
epsilon = 1e-06


def score_chunk(row_tile, cols, start, width):
    return lax.dot_general(
        row_tile,
        cols[pl.ds(start, width), :],
        (((1,), (1,)), ((), ())),
        preferred_element_type=jnp.float32,
    )


def fold_chunks(best, row_tile, cols, traced=None, first_tile=None, before=None):
    total = cols.shape[0]
    for start in range(0, total, CHUNK):
        width = min(CHUNK, total - start)
        if before is not None:
            before(start + width)
        scores = score_chunk(row_tile, cols, start, width)
        if first_tile is not None and start < SUB:
            row_at = lax.broadcasted_iota(jnp.int32, scores.shape, 0)
            col_at = lax.broadcasted_iota(jnp.int32, scores.shape, 1) + start
            same = (row_at == col_at) & (col_at < SUB) & first_tile
            scores = jnp.where(same, -2.0, scores)
        if traced is not None and start < traced.shape[1]:
            traced[:, pl.ds(start, width)] = jnp.maximum(
                traced[:, pl.ds(start, width)], jnp.max(scores, axis=0, keepdims=True)
            )
        for lane in range(0, width, 128):
            piece = scores[:, lane : lane + 128]
            best = piece if best is None else jnp.maximum(best, piece)
    return best


def over_lanes(best):
    return jnp.max(best.T, axis=0, keepdims=True)


def copies_in(refs, target, sems):
    height = refs[0].shape[0]
    copies = [
        pltpu.make_async_copy(ref, target.at[pl.ds(block * height, height)], sems.at[block])
        for block, ref in enumerate(refs)
    ]
    for copy in copies:
        copy.start()
    return copies


def tile_of(array, index, size):
    return array[pl.ds(pl.multiple_of(index * size, size), size), :]


def near_kernel(*refs):
    row_refs, col_refs = refs[:NEAR], refs[NEAR : NEAR + 3]
    lanes_out, rows, cols, row_sems, col_sems = refs[NEAR + 3 :]
    col_copies = copies_in(col_refs, cols, col_sems)
    copies_in(row_refs, rows, row_sems)
    for copy in col_copies:
        copy.wait()
    blocks = 3

    @pl.loop(0, NEAR // blocks)
    def _(index):
        for part in range(blocks):
            block = index * blocks + part
            pltpu.make_async_copy(row_refs[0], rows.at[pl.ds(block * SUB, SUB)], row_sems.at[block]).wait()
        size = blocks * SUB
        best = fold_chunks(None, tile_of(rows, index, size), cols.at[pl.ds(0, EARLY)], first_tile=index == 0)
        lanes_out[pl.ds(pl.multiple_of(index * size, size), size), :] = best


def mid_kernel(*refs):
    row_refs, col_refs = refs[:4], refs[4:7]
    _, _, lanes_out, rows_out, lanes, rows, cols, row_sems, col_sems, out_sems = refs[7:]
    for copy in copies_in(col_refs, cols, col_sems) + copies_in(row_refs, rows, row_sems):
        copy.wait()
    at = pl.ds(NEAR * SUB, PAIR)
    rows_copy = pltpu.make_async_copy(rows, rows_out.at[at], out_sems.at[0])
    rows_copy.start()
    lanes[...] = fold_chunks(None, rows[...], cols.at[pl.ds(0, EARLY)])
    lanes_copy = pltpu.make_async_copy(lanes, lanes_out.at[at], out_sems.at[1])
    lanes_copy.start()
    rows_copy.wait()
    lanes_copy.wait()


def last_kernel(*refs):
    last_refs, first_ref = refs[:3], refs[3]
    lanes, rows, best_out, col_out, cols, sems = refs[4:]
    copies = copies_in(last_refs, cols, sems)
    rest = 3 * SUB - EARLY
    copies.append(
        pltpu.make_async_copy(first_ref.at[pl.ds(SUB - rest, rest)], cols.at[pl.ds(3 * SUB, rest)], sems.at[3])
    )
    copies[-1].start()
    col_out[...] = jnp.full(col_out.shape, -2.0, jnp.float32)
    size = 2 * PAIR

    @pl.loop(0, rows.shape[0] // size)
    def _(index):
        waiting = list(enumerate(copies))

        def before(needed):
            while waiting and waiting[0][0] * SUB < needed:
                copy = waiting.pop(0)[1]
                pl.when(index == 0)(copy.wait)

        lanes_tile = lanes[pl.ds(pl.multiple_of(index * size, size), size), :]
        best = fold_chunks(lanes_tile, tile_of(rows, index, size), cols, traced=col_out, before=before)
        best = over_lanes(best)
        for half in range(2):
            order = index * 2 + half
            distance = jnp.where(order == 1, 3, jnp.where(order == 2, 1, jnp.where(order == 3, 2, 0)))
            for core in range(2):
                begin = half * PAIR + core * SUB
                best_out[core, distance] = best[:, begin : begin + SUB]


ANYWHERE = pl.BlockSpec(memory_space=pl.ANY)
WHOLE = pl.BlockSpec(memory_space=pltpu.VMEM)


def run_kernel(kernel, out_shape, anywhere, whole, scratch, products, aliases=None):
    width = anywhere[0].shape[1]
    return pl.pallas_call(
        kernel,
        out_shape=out_shape,
        in_specs=[ANYWHERE] * len(anywhere) + [WHOLE] * len(whole),
        out_specs=[ANYWHERE if aliases else WHOLE] * len(out_shape),
        scratch_shapes=scratch,
        input_output_aliases=aliases or {},
        cost_estimate=pl.CostEstimate(
            flops=2 * products * SUB * SUB * width, bytes_accessed=products * SUB * width // 2, transcendentals=0
        ),
        compiler_params=pltpu.CompilerParams(vmem_limit_bytes=20 * 2**20),
    )(*anywhere, *whole)


def near_maxima(row_blocks, columns):
    width = columns[0].shape[1]
    total = len(row_blocks) * SUB + PAIR
    return run_kernel(
        near_kernel,
        [jax.ShapeDtypeStruct((total, 128), jnp.float32), jax.ShapeDtypeStruct((total, width), jnp.bfloat16)],
        [*row_blocks, *columns],
        [],
        [
            pltpu.VMEM((len(columns) * SUB, width), jnp.bfloat16),
            pltpu.SemaphoreType.DMA((len(row_blocks),)),
            pltpu.SemaphoreType.DMA((len(columns),)),
        ],
        len(row_blocks) * len(columns),
    )


def mid_maxima(row_blocks, columns, lanes, rows):
    width = columns[0].shape[1]
    count = len(row_blocks) + len(columns)
    return run_kernel(
        mid_kernel,
        [jax.ShapeDtypeStruct(lanes.shape, lanes.dtype), jax.ShapeDtypeStruct(rows.shape, rows.dtype)],
        [*row_blocks, *columns, lanes, rows],
        [],
        [
            pltpu.VMEM((PAIR, 128), jnp.float32),
            pltpu.VMEM((PAIR, width), jnp.bfloat16),
            pltpu.VMEM((len(columns) * SUB, width), jnp.bfloat16),
            pltpu.SemaphoreType.DMA((len(row_blocks),)),
            pltpu.SemaphoreType.DMA((len(columns),)),
            pltpu.SemaphoreType.DMA((2,)),
        ],
        2 * len(columns),
        {count: 0, count + 1: 1},
    )


def last_maxima(columns, first_column, lanes, rows):
    return run_kernel(
        last_kernel,
        [jax.ShapeDtypeStruct((2, 4, 1, SUB), jnp.float32), jax.ShapeDtypeStruct((1, PAIR), jnp.float32)],
        [*columns, first_column],
        [lanes, rows],
        [pltpu.VMEM((6 * SUB - EARLY, rows.shape[1]), jnp.bfloat16), pltpu.SemaphoreType.DMA((4,))],
        24,
    )


def pack_kernel(capacity, owners, values_ref, rows_ref, send_ref, rows, picked, sem):
    copy = pltpu.make_async_copy(rows_ref, rows, sem)
    copy.start()
    lanes = lax.axis_size("tj")
    cluster = BLK * lax.axis_size("ti")
    count, features = rows.shape
    values = values_ref[...]
    member = values >= 0
    grp = jnp.where(values >= cluster, 1, 0)
    inside = values - grp * cluster - lax.axis_index("ti") * BLK
    part = jnp.zeros_like(inside)
    for step in range(1, lanes):
        part = part + jnp.where(inside >= step * SUB, 1, 0)
    code = inside - part * SUB + 1
    owner = jnp.where(member, grp * lanes + part, -1)
    owned = lax.broadcasted_iota(jnp.int32, (owners, count), 0) == owner
    owned_one = jnp.where(owned, 1.0, 0.0)
    block_shape = (BLOCK, BLOCK)
    before = lax.broadcasted_iota(jnp.int32, block_shape, 0) < lax.broadcasted_iota(jnp.int32, block_shape, 1)
    before = jnp.where(before, 1.0, 0.0).astype(jnp.bfloat16)
    so_far = jnp.zeros((owners, 1), jnp.float32)
    ranks = []
    for start in range(0, count, BLOCK):
        part_one = owned_one[:, start : start + BLOCK]
        ranks.append(jnp.dot(part_one.astype(jnp.bfloat16), before, preferred_element_type=jnp.float32) + so_far)
        so_far = so_far + jnp.sum(part_one, axis=1, keepdims=True)
    ranks = jnp.concatenate(ranks, axis=1)
    rank = jnp.sum(jnp.where(owned, ranks, 0.0), axis=0, keepdims=True).astype(jnp.int32)
    slot = jnp.where(member, owner * capacity + rank, -1)
    tag_at = lax.broadcasted_iota(jnp.int32, (TAGS, count), 0)
    low_part = code & 15
    tags = jnp.where(tag_at == 0, code - low_part, jnp.where(tag_at == 1, low_part, 0))
    tags = tags.astype(jnp.float32).astype(jnp.bfloat16)
    for start in range(0, owners * capacity, CHUNK):
        at = lax.broadcasted_iota(jnp.int32, (CHUNK, count), 0) + start
        picked[pl.ds(start, CHUNK), :] = jnp.where(at == slot, 1.0, 0.0).astype(jnp.bfloat16)
    places = lax.dot_general(picked[...], tags, (((1,), (1,)), ((), ())), preferred_element_type=jnp.float32)
    send_ref[:, features:] = places.astype(jnp.bfloat16)
    copy.wait()

    @pl.loop(0, features // CHUNK)
    def _(step):
        at = pl.ds(pl.multiple_of(step * CHUNK, CHUNK), CHUNK)
        taken = jnp.dot(picked[...], rows[:, at], preferred_element_type=jnp.float32)
        send_ref[:, at] = taken.astype(jnp.bfloat16)


def pack_rows(values, rows, capacity, owners):
    count, features = rows.shape
    return pl.pallas_call(
        functools.partial(pack_kernel, capacity, owners),
        out_shape=jax.ShapeDtypeStruct((owners * capacity, features + TAGS), jnp.bfloat16),
        in_specs=[WHOLE, ANYWHERE],
        out_specs=WHOLE,
        scratch_shapes=[
            pltpu.VMEM((count, features), jnp.bfloat16),
            pltpu.VMEM((owners * capacity, count), jnp.bfloat16),
            pltpu.SemaphoreType.DMA,
        ],
        cost_estimate=pl.CostEstimate(
            flops=2 * owners * capacity * count * features, bytes_accessed=4 * count * features, transcendentals=0
        ),
        compiler_params=pltpu.CompilerParams(vmem_limit_bytes=56 * 2**20),
    )(values, rows)


def per_device(corpus, slot_of_row):
    rows_in = corpus[0]
    src_count, features = rows_in.shape
    lanes = lax.axis_size("tj")
    sub_rows = src_count // 2
    capacity = BLK // (lanes * lanes)
    owners = 2 * lanes
    send = pack_rows(slot_of_row, rows_in, capacity, owners).reshape(owners, capacity, features + TAGS)
    got = lax.all_to_all(send, ("grp", "tj"), 0, 0, tiled=True).reshape(owners * capacity, features + TAGS)
    sum_tags = jnp.where(jnp.arange(TAGS, dtype=jnp.int32)[None, :] < 2, 1.0, 0.0).astype(jnp.bfloat16)
    got_places = lax.dot_general(
        sum_tags, got[:, features:], (((1,), (1,)), ((), ())), preferred_element_type=jnp.float32
    )
    wanted = jnp.arange(1, sub_rows + 1, dtype=jnp.int32)[:, None]
    place = (got_places.astype(jnp.int32) == wanted).astype(jnp.bfloat16)
    arrived = jnp.dot(place, got[:, :features], preferred_element_type=jnp.float32)
    row_squares = jnp.sum(arrived * arrived, axis=1, keepdims=True)
    own = (arrived * lax.rsqrt(row_squares + epsilon)).astype(jnp.bfloat16)

    def along_rows(value, pairs):
        return lax.ppermute(value, "ti", pairs)

    def along_cols(value, pairs):
        return lax.ppermute(value, "tj", pairs)

    size = lax.axis_size("ti")
    up = [(i, (i + 2) % size) for i in range(size)]
    down = [(i, (i - 2) % size) for i in range(size)]
    far = [(i, (i + 4) % size) for i in range(size)]
    swap = [(i, i ^ 1) for i in range(size)]
    twin = along_cols(own, swap)
    beside = along_rows(own, swap)
    across = along_rows(own, far)
    low = along_cols(own, up)
    high = along_cols(own, down)

    later, across = lax.optimization_barrier((own, across))
    low_twin = along_cols(low, swap)
    high_twin = along_cols(high, swap)
    half = sub_rows // 2
    mid_top = along_cols(low[:half], up)
    mid_bottom = along_cols(high[half:], down)
    after = along_rows(later, down)
    beside_before = along_rows(beside, up)
    beside_across = along_rows(across, swap)

    lanes_best, rows = near_maxima([own, twin, low, low_twin, high, high_twin], [own, beside, across])
    mid_top, mid_bottom, lanes_best = lax.optimization_barrier((mid_top, mid_bottom, lanes_best))
    mid = [mid_top, mid_bottom, along_cols(mid_top, swap), along_cols(mid_bottom, swap)]
    lanes_best, rows = mid_maxima(mid, [own, beside, across], lanes_best, rows)
    row_best, col_best = last_maxima([after, beside_before, beside_across], across, lanes_best, rows)
    col_best = col_best.reshape(2, sub_rows)
    from_before = along_rows(col_best[:1], up)
    from_beside = along_rows(col_best[1:], [(i, ((i ^ 1) - 2) % size) for i in range(size)])
    twin_best = along_cols(row_best[1], swap)
    chip_best = jnp.maximum(row_best[0], twin_best)
    best = jnp.maximum(chip_best[0], jnp.maximum(from_before, from_beside))
    for step in range(1, lanes // 2):
        best = jnp.maximum(best, along_cols(chip_best[step], [(j, (j + 2 * step) % lanes) for j in range(lanes)]))
    return best


def solution(mesh):
    in_specs = (P("grp", ("ti", "tj"), None), P("grp", ("ti", "tj")))
    out_specs = P("grp", ("ti", "tj"))
    return jax.shard_map(
        per_device, mesh=mesh, in_specs=in_specs, out_specs=out_specs, check_vma=False
    )
```

```python
import functools

import jax
import jax.numpy as jnp
from jax import lax
from jax.experimental import pallas as pl
from jax.experimental.pallas import tpu as pltpu
from jax.sharding import PartitionSpec as P

BLK = 3072
SUB = 384
PAIR = 2 * SUB
CHUNK = 256
NEAR = 6
EARLY = 1024
TAGS = 128
BLOCK = 128
epsilon = 1e-06


def score_chunk(row_tile, cols, start, width):
    return lax.dot_general(
        row_tile,
        cols[pl.ds(start, width), :],
        (((1,), (1,)), ((), ())),
        preferred_element_type=jnp.float32,
    )


def fold_chunks(best, row_tile, cols, traced=None, first_tile=None):
    total = cols.shape[0]
    for start in range(0, total, CHUNK):
        width = min(CHUNK, total - start)
        scores = score_chunk(row_tile, cols, start, width)
        if first_tile is not None and start < SUB:
            row_at = lax.broadcasted_iota(jnp.int32, scores.shape, 0)
            col_at = lax.broadcasted_iota(jnp.int32, scores.shape, 1) + start
            same = (row_at == col_at) & (col_at < SUB) & first_tile
            scores = jnp.where(same, -2.0, scores)
        if traced is not None and start < traced.shape[1]:
            traced[:, pl.ds(start, width)] = jnp.maximum(
                traced[:, pl.ds(start, width)], jnp.max(scores, axis=0, keepdims=True)
            )
        for lane in range(0, width, 128):
            piece = scores[:, lane : lane + 128]
            best = piece if best is None else jnp.maximum(best, piece)
    return best


def over_lanes(best):
    return jnp.max(best.T, axis=0, keepdims=True)


def copies_in(refs, target, sems):
    height = refs[0].shape[0]
    copies = [
        pltpu.make_async_copy(ref, target.at[pl.ds(block * height, height)], sems.at[block])
        for block, ref in enumerate(refs)
    ]
    for copy in copies:
        copy.start()
    return copies


def tile_of(array, index, size):
    return array[pl.ds(pl.multiple_of(index * size, size), size), :]


def near_kernel(*refs):
    row_refs, col_refs = refs[:NEAR], refs[NEAR : NEAR + 3]
    lanes_out, rows, cols, row_sems, col_sems = refs[NEAR + 3 :]
    col_copies = copies_in(col_refs, cols, col_sems)
    copies_in(row_refs, rows, row_sems)
    for copy in col_copies:
        copy.wait()
    blocks = 3

    @pl.loop(0, NEAR // blocks)
    def _(index):
        for part in range(blocks):
            block = index * blocks + part
            pltpu.make_async_copy(row_refs[0], rows.at[pl.ds(block * SUB, SUB)], row_sems.at[block]).wait()
        size = blocks * SUB
        best = fold_chunks(None, tile_of(rows, index, size), cols.at[pl.ds(0, EARLY)], first_tile=index == 0)
        lanes_out[pl.ds(pl.multiple_of(index * size, size), size), :] = best


def mid_kernel(*refs):
    row_refs, col_refs = refs[:4], refs[4:7]
    _, _, lanes_out, rows_out, lanes, rows, cols, row_sems, col_sems, out_sems = refs[7:]
    for copy in copies_in(col_refs, cols, col_sems) + copies_in(row_refs, rows, row_sems):
        copy.wait()
    at = pl.ds(NEAR * SUB, PAIR)
    rows_copy = pltpu.make_async_copy(rows, rows_out.at[at], out_sems.at[0])
    rows_copy.start()
    lanes[...] = fold_chunks(None, rows[...], cols.at[pl.ds(0, EARLY)])
    lanes_copy = pltpu.make_async_copy(lanes, lanes_out.at[at], out_sems.at[1])
    lanes_copy.start()
    rows_copy.wait()
    lanes_copy.wait()


def last_kernel(*refs):
    last_refs, first_ref = refs[:3], refs[3]
    lanes, rows, best_out, col_out, cols, sems = refs[4:]
    copies = copies_in(last_refs, cols, sems)
    rest = 3 * SUB - EARLY
    copies.append(
        pltpu.make_async_copy(first_ref.at[pl.ds(SUB - rest, rest)], cols.at[pl.ds(3 * SUB, rest)], sems.at[3])
    )
    copies[-1].start()
    for copy in copies:
        copy.wait()
    col_out[...] = jnp.full(col_out.shape, -2.0, jnp.float32)
    best = over_lanes(fold_chunks(lanes[...], rows[...], cols, traced=col_out))
    for order, distance in enumerate((0, 3, 1, 2)):
        for core in range(2):
            begin = order * PAIR + core * SUB
            best_out[core, distance] = best[:, begin : begin + SUB]


ANYWHERE = pl.BlockSpec(memory_space=pl.ANY)
WHOLE = pl.BlockSpec(memory_space=pltpu.VMEM)


def run_kernel(kernel, out_shape, anywhere, whole, scratch, products, aliases=None):
    width = anywhere[0].shape[1]
    return pl.pallas_call(
        kernel,
        out_shape=out_shape,
        in_specs=[ANYWHERE] * len(anywhere) + [WHOLE] * len(whole),
        out_specs=[ANYWHERE if aliases else WHOLE] * len(out_shape),
        scratch_shapes=scratch,
        input_output_aliases=aliases or {},
        cost_estimate=pl.CostEstimate(
            flops=2 * products * SUB * SUB * width, bytes_accessed=products * SUB * width // 2, transcendentals=0
        ),
        compiler_params=pltpu.CompilerParams(vmem_limit_bytes=36 * 2**20),
    )(*anywhere, *whole)


def near_maxima(row_blocks, columns):
    width = columns[0].shape[1]
    total = len(row_blocks) * SUB + PAIR
    return run_kernel(
        near_kernel,
        [jax.ShapeDtypeStruct((total, 128), jnp.float32), jax.ShapeDtypeStruct((total, width), jnp.bfloat16)],
        [*row_blocks, *columns],
        [],
        [
            pltpu.VMEM((len(columns) * SUB, width), jnp.bfloat16),
            pltpu.SemaphoreType.DMA((len(row_blocks),)),
            pltpu.SemaphoreType.DMA((len(columns),)),
        ],
        len(row_blocks) * len(columns),
    )


def mid_maxima(row_blocks, columns, lanes, rows):
    width = columns[0].shape[1]
    count = len(row_blocks) + len(columns)
    return run_kernel(
        mid_kernel,
        [jax.ShapeDtypeStruct(lanes.shape, lanes.dtype), jax.ShapeDtypeStruct(rows.shape, rows.dtype)],
        [*row_blocks, *columns, lanes, rows],
        [],
        [
            pltpu.VMEM((PAIR, 128), jnp.float32),
            pltpu.VMEM((PAIR, width), jnp.bfloat16),
            pltpu.VMEM((len(columns) * SUB, width), jnp.bfloat16),
            pltpu.SemaphoreType.DMA((len(row_blocks),)),
            pltpu.SemaphoreType.DMA((len(columns),)),
            pltpu.SemaphoreType.DMA((2,)),
        ],
        2 * len(columns),
        {count: 0, count + 1: 1},
    )


def last_maxima(columns, first_column, lanes, rows):
    return run_kernel(
        last_kernel,
        [jax.ShapeDtypeStruct((2, 4, 1, SUB), jnp.float32), jax.ShapeDtypeStruct((1, PAIR), jnp.float32)],
        [*columns, first_column],
        [lanes, rows],
        [pltpu.VMEM((6 * SUB - EARLY, rows.shape[1]), jnp.bfloat16), pltpu.SemaphoreType.DMA((4,))],
        24,
    )


def pack_kernel(capacity, owners, values_ref, rows_ref, send_ref, rows, picked, sem):
    copy = pltpu.make_async_copy(rows_ref, rows, sem)
    copy.start()
    lanes = lax.axis_size("tj")
    cluster = BLK * lax.axis_size("ti")
    count, features = rows.shape
    values = values_ref[...]
    member = values >= 0
    grp = jnp.where(values >= cluster, 1, 0)
    inside = values - grp * cluster - lax.axis_index("ti") * BLK
    part = jnp.zeros_like(inside)
    for step in range(1, lanes):
        part = part + jnp.where(inside >= step * SUB, 1, 0)
    code = inside - part * SUB + 1
    owner = jnp.where(member, grp * lanes + part, -1)
    owned = lax.broadcasted_iota(jnp.int32, (owners, count), 0) == owner
    owned_one = jnp.where(owned, 1.0, 0.0)
    block_shape = (BLOCK, BLOCK)
    before = lax.broadcasted_iota(jnp.int32, block_shape, 0) < lax.broadcasted_iota(jnp.int32, block_shape, 1)
    before = jnp.where(before, 1.0, 0.0).astype(jnp.bfloat16)
    so_far = jnp.zeros((owners, 1), jnp.float32)
    ranks = []
    for start in range(0, count, BLOCK):
        part_one = owned_one[:, start : start + BLOCK]
        ranks.append(jnp.dot(part_one.astype(jnp.bfloat16), before, preferred_element_type=jnp.float32) + so_far)
        so_far = so_far + jnp.sum(part_one, axis=1, keepdims=True)
    ranks = jnp.concatenate(ranks, axis=1)
    rank = jnp.sum(jnp.where(owned, ranks, 0.0), axis=0, keepdims=True).astype(jnp.int32)
    slot = jnp.where(member, owner * capacity + rank, -1)
    tag_at = lax.broadcasted_iota(jnp.int32, (TAGS, count), 0)
    low_part = code & 15
    tags = jnp.where(tag_at == 0, code - low_part, jnp.where(tag_at == 1, low_part, 0))
    tags = tags.astype(jnp.float32).astype(jnp.bfloat16)
    for start in range(0, owners * capacity, CHUNK):
        at = lax.broadcasted_iota(jnp.int32, (CHUNK, count), 0) + start
        picked[pl.ds(start, CHUNK), :] = jnp.where(at == slot, 1.0, 0.0).astype(jnp.bfloat16)
    places = lax.dot_general(picked[...], tags, (((1,), (1,)), ((), ())), preferred_element_type=jnp.float32)
    send_ref[:, features:] = places.astype(jnp.bfloat16)
    copy.wait()

    @pl.loop(0, features // CHUNK)
    def _(step):
        at = pl.ds(pl.multiple_of(step * CHUNK, CHUNK), CHUNK)
        taken = jnp.dot(picked[...], rows[:, at], preferred_element_type=jnp.float32)
        send_ref[:, at] = taken.astype(jnp.bfloat16)


def pack_rows(values, rows, capacity, owners):
    count, features = rows.shape
    return pl.pallas_call(
        functools.partial(pack_kernel, capacity, owners),
        out_shape=jax.ShapeDtypeStruct((owners * capacity, features + TAGS), jnp.bfloat16),
        in_specs=[WHOLE, ANYWHERE],
        out_specs=WHOLE,
        scratch_shapes=[
            pltpu.VMEM((count, features), jnp.bfloat16),
            pltpu.VMEM((owners * capacity, count), jnp.bfloat16),
            pltpu.SemaphoreType.DMA,
        ],
        cost_estimate=pl.CostEstimate(
            flops=2 * owners * capacity * count * features, bytes_accessed=4 * count * features, transcendentals=0
        ),
        compiler_params=pltpu.CompilerParams(vmem_limit_bytes=56 * 2**20),
    )(values, rows)


def per_device(corpus, slot_of_row):
    rows_in = corpus[0]
    src_count, features = rows_in.shape
    lanes = lax.axis_size("tj")
    sub_rows = src_count // 2
    capacity = BLK // (lanes * lanes)
    owners = 2 * lanes
    send = pack_rows(slot_of_row, rows_in, capacity, owners).reshape(owners, capacity, features + TAGS)
    got = lax.all_to_all(send, ("grp", "tj"), 0, 0, tiled=True).reshape(owners * capacity, features + TAGS)
    sum_tags = jnp.where(jnp.arange(TAGS, dtype=jnp.int32)[None, :] < 2, 1.0, 0.0).astype(jnp.bfloat16)
    got_places = lax.dot_general(
        sum_tags, got[:, features:], (((1,), (1,)), ((), ())), preferred_element_type=jnp.float32
    )
    wanted = jnp.arange(1, sub_rows + 1, dtype=jnp.int32)[:, None]
    place = (got_places.astype(jnp.int32) == wanted).astype(jnp.bfloat16)
    arrived = jnp.dot(place, got[:, :features], preferred_element_type=jnp.float32)
    row_squares = jnp.sum(arrived * arrived, axis=1, keepdims=True)
    own = (arrived * lax.rsqrt(row_squares + epsilon)).astype(jnp.bfloat16)

    def along_rows(value, pairs):
        return lax.ppermute(value, "ti", pairs)

    def along_cols(value, pairs):
        return lax.ppermute(value, "tj", pairs)

    size = lax.axis_size("ti")
    up = [(i, (i + 2) % size) for i in range(size)]
    down = [(i, (i - 2) % size) for i in range(size)]
    far = [(i, (i + 4) % size) for i in range(size)]
    swap = [(i, i ^ 1) for i in range(size)]
    twin = along_cols(own, swap)
    beside = along_rows(own, swap)
    across = along_rows(own, far)
    low = along_cols(own, up)
    high = along_cols(own, down)

    later, across = lax.optimization_barrier((own, across))
    low_twin = along_cols(low, swap)
    high_twin = along_cols(high, swap)
    half = sub_rows // 2
    mid_top = along_cols(low[:half], up)
    mid_bottom = along_cols(high[half:], down)
    after = along_rows(later, down)
    beside_before = along_rows(beside, up)
    beside_across = along_rows(across, swap)

    lanes_best, rows = near_maxima([own, twin, low, low_twin, high, high_twin], [own, beside, across])
    mid_top, mid_bottom, lanes_best = lax.optimization_barrier((mid_top, mid_bottom, lanes_best))
    mid = [mid_top, mid_bottom, along_cols(mid_top, swap), along_cols(mid_bottom, swap)]
    lanes_best, rows = mid_maxima(mid, [own, beside, across], lanes_best, rows)
    row_best, col_best = last_maxima([after, beside_before, beside_across], across, lanes_best, rows)
    col_best = col_best.reshape(2, sub_rows)
    from_before = along_rows(col_best[:1], up)
    from_beside = along_rows(col_best[1:], [(i, ((i ^ 1) - 2) % size) for i in range(size)])
    twin_best = along_cols(row_best[1], swap)
    chip_best = jnp.maximum(row_best[0], twin_best)
    best = jnp.maximum(chip_best[0], jnp.maximum(from_before, from_beside))
    for step in range(1, lanes // 2):
        best = jnp.maximum(best, along_cols(chip_best[step], [(j, (j + 2 * step) % lanes) for j in range(lanes)]))
    return best


def solution(mesh):
    in_specs = (P("grp", ("ti", "tj"), None), P("grp", ("ti", "tj")))
    out_specs = P("grp", ("ti", "tj"))
    return jax.shard_map(
        per_device, mesh=mesh, in_specs=in_specs, out_specs=out_specs, check_vma=False
    )
```

```python
import functools

import jax
import jax.numpy as jnp
from jax import lax
from jax.experimental import pallas as pl
from jax.experimental.pallas import tpu as pltpu
from jax.sharding import PartitionSpec as P

BLK = 3072
SUB = 384
PAIR = 2 * SUB
CHUNK = 256
NEAR = 6
EARLY = 1024
TAGS = 128
BLOCK = 128
epsilon = 1e-06


def score_chunk(row_tile, cols, start, width):
    return lax.dot_general(
        row_tile,
        cols[pl.ds(start, width), :],
        (((1,), (1,)), ((), ())),
        preferred_element_type=jnp.float32,
    )


def fold_chunks(best, row_tile, cols, traced=None, first_tile=None):
    total = cols.shape[0]
    for start in range(0, total, CHUNK):
        width = min(CHUNK, total - start)
        scores = score_chunk(row_tile, cols, start, width)
        if first_tile is not None and start < SUB:
            row_at = lax.broadcasted_iota(jnp.int32, scores.shape, 0)
            col_at = lax.broadcasted_iota(jnp.int32, scores.shape, 1) + start
            same = (row_at == col_at) & (col_at < SUB) & first_tile
            scores = jnp.where(same, -2.0, scores)
        if traced is not None and start < traced.shape[1]:
            traced[:, pl.ds(start, width)] = jnp.maximum(
                traced[:, pl.ds(start, width)], jnp.max(scores, axis=0, keepdims=True)
            )
        for lane in range(0, width, 128):
            piece = scores[:, lane : lane + 128]
            best = piece if best is None else jnp.maximum(best, piece)
    return best


def over_lanes(best):
    return jnp.max(best.T, axis=0, keepdims=True)


def copies_in(refs, target, sems):
    height = refs[0].shape[0]
    copies = [
        pltpu.make_async_copy(ref, target.at[pl.ds(block * height, height)], sems.at[block])
        for block, ref in enumerate(refs)
    ]
    for copy in copies:
        copy.start()
    return copies


def tile_of(array, index, size):
    return array[pl.ds(pl.multiple_of(index * size, size), size), :]


def near_kernel(*refs):
    row_refs, col_refs = refs[:NEAR], refs[NEAR : NEAR + 3]
    lanes_out, rows, cols, row_sems, col_sems = refs[NEAR + 3 :]
    col_copies = copies_in(col_refs, cols, col_sems)
    copies_in(row_refs, rows, row_sems)
    for copy in col_copies:
        copy.wait()
    blocks = 3

    @pl.loop(0, NEAR // blocks)
    def _(index):
        for part in range(blocks):
            block = index * blocks + part
            pltpu.make_async_copy(row_refs[0], rows.at[pl.ds(block * SUB, SUB)], row_sems.at[block]).wait()
        size = blocks * SUB
        best = fold_chunks(None, tile_of(rows, index, size), cols.at[pl.ds(0, EARLY)], first_tile=index == 0)
        lanes_out[pl.ds(pl.multiple_of(index * size, size), size), :] = best


def mid_kernel(*refs):
    row_refs, col_refs = refs[:4], refs[4:7]
    _, _, lanes_out, rows_out, lanes, rows, cols, row_sems, col_sems, out_sems = refs[7:]
    for copy in copies_in(col_refs, cols, col_sems) + copies_in(row_refs, rows, row_sems):
        copy.wait()
    at = pl.ds(NEAR * SUB, PAIR)
    rows_copy = pltpu.make_async_copy(rows, rows_out.at[at], out_sems.at[0])
    rows_copy.start()
    lanes[...] = fold_chunks(None, rows[...], cols.at[pl.ds(0, EARLY)])
    lanes_copy = pltpu.make_async_copy(lanes, lanes_out.at[at], out_sems.at[1])
    lanes_copy.start()
    rows_copy.wait()
    lanes_copy.wait()


def last_kernel(*refs):
    last_refs, first_ref = refs[:3], refs[3]
    lanes, rows, best_out, col_out, cols, sems = refs[4:]
    copies = copies_in(last_refs, cols, sems)
    rest = 3 * SUB - EARLY
    copies.append(
        pltpu.make_async_copy(first_ref.at[pl.ds(SUB - rest, rest)], cols.at[pl.ds(3 * SUB, rest)], sems.at[3])
    )
    copies[-1].start()
    for copy in copies:
        copy.wait()
    col_out[...] = jnp.full(col_out.shape, -2.0, jnp.float32)
    best = over_lanes(fold_chunks(lanes[...], rows[...], cols, traced=col_out))
    odd = lax.rem(lax.axis_index("tj") // 2, 2)
    for order, partner in enumerate((0, 3 - 2 * odd, 1 + 2 * odd, 2)):
        for core in range(2):
            begin = order * PAIR + core * SUB
            best_out[core, partner] = best[:, begin : begin + SUB]


ANYWHERE = pl.BlockSpec(memory_space=pl.ANY)
WHOLE = pl.BlockSpec(memory_space=pltpu.VMEM)


def run_kernel(kernel, out_shape, anywhere, whole, scratch, products, aliases=None):
    width = anywhere[0].shape[1]
    return pl.pallas_call(
        kernel,
        out_shape=out_shape,
        in_specs=[ANYWHERE] * len(anywhere) + [WHOLE] * len(whole),
        out_specs=[ANYWHERE if aliases else WHOLE] * len(out_shape),
        scratch_shapes=scratch,
        input_output_aliases=aliases or {},
        cost_estimate=pl.CostEstimate(
            flops=2 * products * SUB * SUB * width, bytes_accessed=products * SUB * width // 2, transcendentals=0
        ),
        compiler_params=pltpu.CompilerParams(vmem_limit_bytes=36 * 2**20),
    )(*anywhere, *whole)


def near_maxima(row_blocks, columns):
    width = columns[0].shape[1]
    total = len(row_blocks) * SUB + PAIR
    return run_kernel(
        near_kernel,
        [jax.ShapeDtypeStruct((total, 128), jnp.float32), jax.ShapeDtypeStruct((total, width), jnp.bfloat16)],
        [*row_blocks, *columns],
        [],
        [
            pltpu.VMEM((len(columns) * SUB, width), jnp.bfloat16),
            pltpu.SemaphoreType.DMA((len(row_blocks),)),
            pltpu.SemaphoreType.DMA((len(columns),)),
        ],
        len(row_blocks) * len(columns),
    )


def mid_maxima(row_blocks, columns, lanes, rows):
    width = columns[0].shape[1]
    count = len(row_blocks) + len(columns)
    return run_kernel(
        mid_kernel,
        [jax.ShapeDtypeStruct(lanes.shape, lanes.dtype), jax.ShapeDtypeStruct(rows.shape, rows.dtype)],
        [*row_blocks, *columns, lanes, rows],
        [],
        [
            pltpu.VMEM((PAIR, 128), jnp.float32),
            pltpu.VMEM((PAIR, width), jnp.bfloat16),
            pltpu.VMEM((len(columns) * SUB, width), jnp.bfloat16),
            pltpu.SemaphoreType.DMA((len(row_blocks),)),
            pltpu.SemaphoreType.DMA((len(columns),)),
            pltpu.SemaphoreType.DMA((2,)),
        ],
        2 * len(columns),
        {count: 0, count + 1: 1},
    )


def last_maxima(columns, first_column, lanes, rows):
    return run_kernel(
        last_kernel,
        [jax.ShapeDtypeStruct((2, 4, 1, SUB), jnp.float32), jax.ShapeDtypeStruct((1, PAIR), jnp.float32)],
        [*columns, first_column],
        [lanes, rows],
        [pltpu.VMEM((6 * SUB - EARLY, rows.shape[1]), jnp.bfloat16), pltpu.SemaphoreType.DMA((4,))],
        24,
    )


def pack_kernel(capacity, owners, values_ref, rows_ref, send_ref, rows, picked, sem):
    copy = pltpu.make_async_copy(rows_ref, rows, sem)
    copy.start()
    lanes = lax.axis_size("tj")
    cluster = BLK * lax.axis_size("ti")
    count, features = rows.shape
    values = values_ref[...]
    member = values >= 0
    grp = jnp.where(values >= cluster, 1, 0)
    inside = values - grp * cluster - lax.axis_index("ti") * BLK
    part = jnp.zeros_like(inside)
    for step in range(1, lanes):
        part = part + jnp.where(inside >= step * SUB, 1, 0)
    code = inside - part * SUB + 1
    owner = jnp.where(member, grp * lanes + part, -1)
    owned = lax.broadcasted_iota(jnp.int32, (owners, count), 0) == owner
    owned_one = jnp.where(owned, 1.0, 0.0)
    block_shape = (BLOCK, BLOCK)
    before = lax.broadcasted_iota(jnp.int32, block_shape, 0) < lax.broadcasted_iota(jnp.int32, block_shape, 1)
    before = jnp.where(before, 1.0, 0.0).astype(jnp.bfloat16)
    so_far = jnp.zeros((owners, 1), jnp.float32)
    ranks = []
    for start in range(0, count, BLOCK):
        part_one = owned_one[:, start : start + BLOCK]
        ranks.append(jnp.dot(part_one.astype(jnp.bfloat16), before, preferred_element_type=jnp.float32) + so_far)
        so_far = so_far + jnp.sum(part_one, axis=1, keepdims=True)
    ranks = jnp.concatenate(ranks, axis=1)
    rank = jnp.sum(jnp.where(owned, ranks, 0.0), axis=0, keepdims=True).astype(jnp.int32)
    slot = jnp.where(member, owner * capacity + rank, -1)
    tag_at = lax.broadcasted_iota(jnp.int32, (TAGS, count), 0)
    low_part = code & 15
    tags = jnp.where(tag_at == 0, code - low_part, jnp.where(tag_at == 1, low_part, 0))
    tags = tags.astype(jnp.float32).astype(jnp.bfloat16)
    for start in range(0, owners * capacity, CHUNK):
        at = lax.broadcasted_iota(jnp.int32, (CHUNK, count), 0) + start
        picked[pl.ds(start, CHUNK), :] = jnp.where(at == slot, 1.0, 0.0).astype(jnp.bfloat16)
    places = lax.dot_general(picked[...], tags, (((1,), (1,)), ((), ())), preferred_element_type=jnp.float32)
    send_ref[:, features:] = places.astype(jnp.bfloat16)
    copy.wait()

    @pl.loop(0, features // CHUNK)
    def _(step):
        at = pl.ds(pl.multiple_of(step * CHUNK, CHUNK), CHUNK)
        taken = jnp.dot(picked[...], rows[:, at], preferred_element_type=jnp.float32)
        send_ref[:, at] = taken.astype(jnp.bfloat16)


def pack_rows(values, rows, capacity, owners):
    count, features = rows.shape
    return pl.pallas_call(
        functools.partial(pack_kernel, capacity, owners),
        out_shape=jax.ShapeDtypeStruct((owners * capacity, features + TAGS), jnp.bfloat16),
        in_specs=[WHOLE, ANYWHERE],
        out_specs=WHOLE,
        scratch_shapes=[
            pltpu.VMEM((count, features), jnp.bfloat16),
            pltpu.VMEM((owners * capacity, count), jnp.bfloat16),
            pltpu.SemaphoreType.DMA,
        ],
        cost_estimate=pl.CostEstimate(
            flops=2 * owners * capacity * count * features, bytes_accessed=4 * count * features, transcendentals=0
        ),
        compiler_params=pltpu.CompilerParams(vmem_limit_bytes=56 * 2**20),
    )(values, rows)


def per_device(corpus, slot_of_row):
    rows_in = corpus[0]
    src_count, features = rows_in.shape
    lanes = lax.axis_size("tj")
    sub_rows = src_count // 2
    capacity = BLK // (lanes * lanes)
    owners = 2 * lanes
    send = pack_rows(slot_of_row, rows_in, capacity, owners).reshape(owners, capacity, features + TAGS)
    got = lax.all_to_all(send, ("grp", "tj"), 0, 0, tiled=True).reshape(owners * capacity, features + TAGS)
    sum_tags = jnp.where(jnp.arange(TAGS, dtype=jnp.int32)[None, :] < 2, 1.0, 0.0).astype(jnp.bfloat16)
    got_places = lax.dot_general(
        sum_tags, got[:, features:], (((1,), (1,)), ((), ())), preferred_element_type=jnp.float32
    )
    wanted = jnp.arange(1, sub_rows + 1, dtype=jnp.int32)[:, None]
    place = (got_places.astype(jnp.int32) == wanted).astype(jnp.bfloat16)
    arrived = jnp.dot(place, got[:, :features], preferred_element_type=jnp.float32)
    row_squares = jnp.sum(arrived * arrived, axis=1, keepdims=True)
    own = (arrived * lax.rsqrt(row_squares + epsilon)).astype(jnp.bfloat16)

    def along_rows(value, pairs):
        return lax.ppermute(value, "ti", pairs)

    def along_cols(value, pairs):
        return lax.ppermute(value, "tj", pairs)

    size = lax.axis_size("ti")
    up = [(i, (i + 2) % size) for i in range(size)]
    down = [(i, (i - 2) % size) for i in range(size)]
    far = [(i, (i + 4) % size) for i in range(size)]
    swap = [(i, i ^ 1) for i in range(size)]
    twin = along_cols(own, swap)
    beside = along_rows(own, swap)
    across = along_rows(own, far)
    low = along_cols(own, up)
    high = along_cols(own, down)

    later, across = lax.optimization_barrier((own, across))
    low_twin = along_cols(low, swap)
    high_twin = along_cols(high, swap)
    half = sub_rows // 2
    mid_top = along_cols(low[:half], up)
    mid_bottom = along_cols(high[half:], down)
    after = along_rows(later, down)
    beside_before = along_rows(beside, up)
    beside_across = along_rows(across, swap)

    lanes_best, rows = near_maxima([own, twin, low, low_twin, high, high_twin], [own, beside, across])
    mid_top, mid_bottom, lanes_best = lax.optimization_barrier((mid_top, mid_bottom, lanes_best))
    mid = [mid_top, mid_bottom, along_cols(mid_top, swap), along_cols(mid_bottom, swap)]
    lanes_best, rows = mid_maxima(mid, [own, beside, across], lanes_best, rows)
    row_best, col_best = last_maxima([after, beside_before, beside_across], across, lanes_best, rows)
    col_best = col_best.reshape(2, sub_rows)
    twin_best = along_cols(row_best[1], swap)
    chip_best = jnp.maximum(row_best[0], twin_best)
    half_best = jnp.maximum(chip_best[:2], along_cols(chip_best[2:], far))
    from_before = along_rows(col_best[:1], up)
    from_beside = along_rows(col_best[1:], [(i, ((i ^ 1) - 2) % size) for i in range(size)])
    beside_z = along_cols(half_best[1], [(j, j ^ 2) for j in range(lanes)])
    best = jnp.maximum(jnp.maximum(half_best[0], beside_z), jnp.maximum(from_before, from_beside))
    return best


def solution(mesh):
    in_specs = (P("grp", ("ti", "tj"), None), P("grp", ("ti", "tj")))
    out_specs = P("grp", ("ti", "tj"))
    return jax.shard_map(
        per_device, mesh=mesh, in_specs=in_specs, out_specs=out_specs, check_vma=False
    )
```

```python
import functools

import jax
import jax.numpy as jnp
from jax import lax
from jax.experimental import pallas as pl
from jax.experimental.pallas import tpu as pltpu
from jax.sharding import PartitionSpec as P

BLK = 3072
SUB = 384
PAIR = 2 * SUB
CHUNK = 256
NEAR = 6
EARLY = 1024
TAGS = 128
BLOCK = 128
epsilon = 1e-06


def score_chunk(row_tile, cols, start, width):
    return lax.dot_general(
        row_tile,
        cols[pl.ds(start, width), :],
        (((1,), (1,)), ((), ())),
        preferred_element_type=jnp.float32,
    )


def fold_chunks(best, row_tile, cols, traced=None, first_tile=None):
    total = cols.shape[0]
    for start in range(0, total, CHUNK):
        width = min(CHUNK, total - start)
        scores = score_chunk(row_tile, cols, start, width)
        if first_tile is not None and start < SUB:
            row_at = lax.broadcasted_iota(jnp.int32, scores.shape, 0)
            col_at = lax.broadcasted_iota(jnp.int32, scores.shape, 1) + start
            same = (row_at == col_at) & (col_at < SUB) & first_tile
            scores = jnp.where(same, -2.0, scores)
        if traced is not None and start < traced.shape[1]:
            traced[:, pl.ds(start, width)] = jnp.maximum(
                traced[:, pl.ds(start, width)], jnp.max(scores, axis=0, keepdims=True)
            )
        for lane in range(0, width, 128):
            piece = scores[:, lane : lane + 128]
            best = piece if best is None else jnp.maximum(best, piece)
    return best


def over_lanes(best):
    return jnp.max(best.T, axis=0, keepdims=True)


def copies_in(refs, target, sems):
    height = refs[0].shape[0]
    copies = [
        pltpu.make_async_copy(ref, target.at[pl.ds(block * height, height)], sems.at[block])
        for block, ref in enumerate(refs)
    ]
    for copy in copies:
        copy.start()
    return copies


def tile_of(array, index, size):
    return array[pl.ds(pl.multiple_of(index * size, size), size), :]


def near_kernel(*refs):
    row_refs, col_refs = refs[:NEAR], refs[NEAR : NEAR + 3]
    lanes_out, rows, cols, row_sems, col_sems = refs[NEAR + 3 :]
    col_copies = copies_in(col_refs, cols, col_sems)
    copies_in(row_refs, rows, row_sems)
    for copy in col_copies:
        copy.wait()
    blocks = 3

    @pl.loop(0, NEAR // blocks)
    def _(index):
        for part in range(blocks):
            block = index * blocks + part
            pltpu.make_async_copy(row_refs[0], rows.at[pl.ds(block * SUB, SUB)], row_sems.at[block]).wait()
        size = blocks * SUB
        best = fold_chunks(None, tile_of(rows, index, size), cols.at[pl.ds(0, EARLY)], first_tile=index == 0)
        lanes_out[pl.ds(pl.multiple_of(index * size, size), size), :] = best


def mid_kernel(*refs):
    row_refs, col_refs = refs[:4], refs[4:7]
    _, _, lanes_out, rows_out, lanes, rows, cols, row_sems, col_sems, out_sems = refs[7:]
    for copy in copies_in(col_refs, cols, col_sems) + copies_in(row_refs, rows, row_sems):
        copy.wait()
    at = pl.ds(NEAR * SUB, PAIR)
    rows_copy = pltpu.make_async_copy(rows, rows_out.at[at], out_sems.at[0])
    rows_copy.start()
    lanes[...] = fold_chunks(None, rows[...], cols.at[pl.ds(0, EARLY)])
    lanes_copy = pltpu.make_async_copy(lanes, lanes_out.at[at], out_sems.at[1])
    lanes_copy.start()
    rows_copy.wait()
    lanes_copy.wait()


def last_kernel(*refs):
    last_refs, first_ref = refs[:3], refs[3]
    lanes, rows, best_out, col_out, cols, sems = refs[4:]
    copies = copies_in(last_refs, cols, sems)
    rest = 3 * SUB - EARLY
    copies.append(
        pltpu.make_async_copy(first_ref.at[pl.ds(SUB - rest, rest)], cols.at[pl.ds(3 * SUB, rest)], sems.at[3])
    )
    copies[-1].start()
    for copy in copies:
        copy.wait()
    col_out[...] = jnp.full(col_out.shape, -2.0, jnp.float32)
    best = over_lanes(fold_chunks(lanes[...], rows[...], cols, traced=col_out))
    for order, distance in enumerate((0, 3, 1, 2)):
        for core in range(2):
            begin = order * PAIR + core * SUB
            best_out[core, distance] = best[:, begin : begin + SUB]


ANYWHERE = pl.BlockSpec(memory_space=pl.ANY)
WHOLE = pl.BlockSpec(memory_space=pltpu.VMEM)


def run_kernel(kernel, out_shape, anywhere, whole, scratch, products, aliases=None):
    width = anywhere[0].shape[1]
    return pl.pallas_call(
        kernel,
        out_shape=out_shape,
        in_specs=[ANYWHERE] * len(anywhere) + [WHOLE] * len(whole),
        out_specs=[ANYWHERE if aliases else WHOLE] * len(out_shape),
        scratch_shapes=scratch,
        input_output_aliases=aliases or {},
        cost_estimate=pl.CostEstimate(
            flops=2 * products * SUB * SUB * width, bytes_accessed=products * SUB * width // 2, transcendentals=0
        ),
        compiler_params=pltpu.CompilerParams(vmem_limit_bytes=36 * 2**20),
    )(*anywhere, *whole)


def near_maxima(row_blocks, columns):
    width = columns[0].shape[1]
    total = len(row_blocks) * SUB + PAIR
    return run_kernel(
        near_kernel,
        [jax.ShapeDtypeStruct((total, 128), jnp.float32), jax.ShapeDtypeStruct((total, width), jnp.bfloat16)],
        [*row_blocks, *columns],
        [],
        [
            pltpu.VMEM((len(columns) * SUB, width), jnp.bfloat16),
            pltpu.SemaphoreType.DMA((len(row_blocks),)),
            pltpu.SemaphoreType.DMA((len(columns),)),
        ],
        len(row_blocks) * len(columns),
    )


def mid_maxima(row_blocks, columns, lanes, rows):
    width = columns[0].shape[1]
    count = len(row_blocks) + len(columns)
    return run_kernel(
        mid_kernel,
        [jax.ShapeDtypeStruct(lanes.shape, lanes.dtype), jax.ShapeDtypeStruct(rows.shape, rows.dtype)],
        [*row_blocks, *columns, lanes, rows],
        [],
        [
            pltpu.VMEM((PAIR, 128), jnp.float32),
            pltpu.VMEM((PAIR, width), jnp.bfloat16),
            pltpu.VMEM((len(columns) * SUB, width), jnp.bfloat16),
            pltpu.SemaphoreType.DMA((len(row_blocks),)),
            pltpu.SemaphoreType.DMA((len(columns),)),
            pltpu.SemaphoreType.DMA((2,)),
        ],
        2 * len(columns),
        {count: 0, count + 1: 1},
    )


def last_maxima(columns, first_column, lanes, rows):
    return run_kernel(
        last_kernel,
        [jax.ShapeDtypeStruct((2, 4, 1, SUB), jnp.float32), jax.ShapeDtypeStruct((1, PAIR), jnp.float32)],
        [*columns, first_column],
        [lanes, rows],
        [pltpu.VMEM((6 * SUB - EARLY, rows.shape[1]), jnp.bfloat16), pltpu.SemaphoreType.DMA((4,))],
        24,
    )


def pack_kernel(capacity, owners, values_ref, rows_ref, send_ref, rows, picked, sem):
    copy = pltpu.make_async_copy(rows_ref, rows, sem)
    copy.start()
    lanes = lax.axis_size("tj")
    cluster = BLK * lax.axis_size("ti")
    count, features = rows.shape
    values = values_ref[...]
    member = values >= 0
    grp = jnp.where(values >= cluster, 1, 0)
    inside = values - grp * cluster - lax.axis_index("ti") * BLK
    part = jnp.zeros_like(inside)
    for step in range(1, lanes):
        part = part + jnp.where(inside >= step * SUB, 1, 0)
    code = inside - part * SUB + 1
    owner = jnp.where(member, grp * lanes + part, -1)
    owned = lax.broadcasted_iota(jnp.int32, (owners, count), 0) == owner
    owned_one = jnp.where(owned, 1.0, 0.0)
    block_shape = (BLOCK, BLOCK)
    before = lax.broadcasted_iota(jnp.int32, block_shape, 0) < lax.broadcasted_iota(jnp.int32, block_shape, 1)
    before = jnp.where(before, 1.0, 0.0).astype(jnp.bfloat16)
    so_far = jnp.zeros((owners, 1), jnp.float32)
    ranks = []
    for start in range(0, count, BLOCK):
        part_one = owned_one[:, start : start + BLOCK]
        ranks.append(jnp.dot(part_one.astype(jnp.bfloat16), before, preferred_element_type=jnp.float32) + so_far)
        so_far = so_far + jnp.sum(part_one, axis=1, keepdims=True)
    ranks = jnp.concatenate(ranks, axis=1)
    rank = jnp.sum(jnp.where(owned, ranks, 0.0), axis=0, keepdims=True).astype(jnp.int32)
    slot = jnp.where(member, owner * capacity + rank, -1)
    tag_at = lax.broadcasted_iota(jnp.int32, (TAGS, count), 0)
    low_part = code & 15
    tags = jnp.where(tag_at == 0, code - low_part, jnp.where(tag_at == 1, low_part, 0))
    tags = tags.astype(jnp.float32).astype(jnp.bfloat16)
    for start in range(0, owners * capacity, CHUNK):
        at = lax.broadcasted_iota(jnp.int32, (CHUNK, count), 0) + start
        picked[pl.ds(start, CHUNK), :] = jnp.where(at == slot, 1.0, 0.0).astype(jnp.bfloat16)
    places = lax.dot_general(picked[...], tags, (((1,), (1,)), ((), ())), preferred_element_type=jnp.float32)
    send_ref[:, features:] = places.astype(jnp.bfloat16)
    copy.wait()

    @pl.loop(0, features // CHUNK)
    def _(step):
        at = pl.ds(pl.multiple_of(step * CHUNK, CHUNK), CHUNK)
        taken = jnp.dot(picked[...], rows[:, at], preferred_element_type=jnp.float32)
        send_ref[:, at] = taken.astype(jnp.bfloat16)


def pack_rows(values, rows, capacity, owners):
    count, features = rows.shape
    return pl.pallas_call(
        functools.partial(pack_kernel, capacity, owners),
        out_shape=jax.ShapeDtypeStruct((owners * capacity, features + TAGS), jnp.bfloat16),
        in_specs=[WHOLE, ANYWHERE],
        out_specs=WHOLE,
        scratch_shapes=[
            pltpu.VMEM((count, features), jnp.bfloat16),
            pltpu.VMEM((owners * capacity, count), jnp.bfloat16),
            pltpu.SemaphoreType.DMA,
        ],
        cost_estimate=pl.CostEstimate(
            flops=2 * owners * capacity * count * features, bytes_accessed=4 * count * features, transcendentals=0
        ),
        compiler_params=pltpu.CompilerParams(vmem_limit_bytes=56 * 2**20),
    )(values, rows)


def per_device(corpus, slot_of_row):
    rows_in = corpus[0]
    src_count, features = rows_in.shape
    lanes = lax.axis_size("tj")
    sub_rows = src_count // 2
    capacity = BLK // (lanes * lanes)
    owners = 2 * lanes
    send = pack_rows(slot_of_row, rows_in, capacity, owners).reshape(owners, capacity, features + TAGS)
    got = lax.all_to_all(send, ("grp", "tj"), 0, 0, tiled=True).reshape(owners * capacity, features + TAGS)
    sum_tags = jnp.where(jnp.arange(TAGS, dtype=jnp.int32)[None, :] < 2, 1.0, 0.0).astype(jnp.bfloat16)
    got_places = lax.dot_general(
        sum_tags, got[:, features:], (((1,), (1,)), ((), ())), preferred_element_type=jnp.float32
    )
    wanted = jnp.arange(1, sub_rows + 1, dtype=jnp.int32)[:, None]
    place = (got_places.astype(jnp.int32) == wanted).astype(jnp.bfloat16)
    arrived = jnp.dot(place, got[:, :features], preferred_element_type=jnp.float32)
    row_squares = jnp.sum(arrived * arrived, axis=1, keepdims=True)
    own = (arrived * lax.rsqrt(row_squares + epsilon)).astype(jnp.bfloat16)

    def along_rows(value, pairs):
        return lax.ppermute(value, "ti", pairs)

    def along_cols(value, pairs):
        return lax.ppermute(value, "tj", pairs)

    size = lax.axis_size("ti")
    up = [(i, (i + 2) % size) for i in range(size)]
    down = [(i, (i - 2) % size) for i in range(size)]
    far = [(i, (i + 4) % size) for i in range(size)]
    swap = [(i, i ^ 1) for i in range(size)]
    twin = along_cols(own, swap)
    beside = along_rows(own, swap)
    across = along_rows(own, far)
    low = along_cols(own, up)
    high = along_cols(own, down)

    later, across = lax.optimization_barrier((own, across))
    low_twin = along_cols(low, swap)
    high_twin = along_cols(high, swap)
    half = sub_rows // 2
    low_half, high_half, low_twin, high_twin = lax.optimization_barrier((low[:half], high[half:], low_twin, high_twin))
    mid_top = along_cols(low_half, up)
    mid_bottom = along_cols(high_half, down)
    after = along_rows(later, down)
    beside_before = along_rows(beside, up)
    beside_across = along_rows(across, swap)

    lanes_best, rows = near_maxima([own, twin, low, low_twin, high, high_twin], [own, beside, across])
    mid_top, mid_bottom, lanes_best = lax.optimization_barrier((mid_top, mid_bottom, lanes_best))
    mid = [mid_top, mid_bottom, along_cols(mid_top, swap), along_cols(mid_bottom, swap)]
    lanes_best, rows = mid_maxima(mid, [own, beside, across], lanes_best, rows)
    row_best, col_best = last_maxima([after, beside_before, beside_across], across, lanes_best, rows)
    col_best = col_best.reshape(2, sub_rows)
    from_before = along_rows(col_best[:1], up)
    from_beside = along_rows(col_best[1:], [(i, ((i ^ 1) - 2) % size) for i in range(size)])
    twin_best = along_cols(row_best[1], swap)
    chip_best = jnp.maximum(row_best[0], twin_best)
    best = jnp.maximum(chip_best[0], jnp.maximum(from_before, from_beside))
    for step in range(1, lanes // 2):
        best = jnp.maximum(best, along_cols(chip_best[step], [(j, (j + 2 * step) % lanes) for j in range(lanes)]))
    return best


def solution(mesh):
    in_specs = (P("grp", ("ti", "tj"), None), P("grp", ("ti", "tj")))
    out_specs = P("grp", ("ti", "tj"))
    return jax.shard_map(
        per_device, mesh=mesh, in_specs=in_specs, out_specs=out_specs, check_vma=False
    )
```

```python
import functools

import jax
import jax.numpy as jnp
from jax import lax
from jax.experimental import pallas as pl
from jax.experimental.pallas import tpu as pltpu
from jax.sharding import PartitionSpec as P

BLK = 3072
SUB = 384
PAIR = 2 * SUB
CHUNK = 256
NEAR = 6
TAGS = 128
BLOCK = 128
epsilon = 1e-06


def score_chunk(row_tile, cols, start, width):
    return lax.dot_general(
        row_tile,
        cols[pl.ds(start, width), :],
        (((1,), (1,)), ((), ())),
        preferred_element_type=jnp.float32,
    )


def fold_chunks(best, row_tile, cols, traced=None, first_tile=None):
    total = cols.shape[0]
    for start in range(0, total, CHUNK):
        width = min(CHUNK, total - start)
        scores = score_chunk(row_tile, cols, start, width)
        if first_tile is not None and start < SUB:
            row_at = lax.broadcasted_iota(jnp.int32, scores.shape, 0)
            col_at = lax.broadcasted_iota(jnp.int32, scores.shape, 1) + start
            same = (row_at == col_at) & (col_at < SUB) & first_tile
            scores = jnp.where(same, -2.0, scores)
        if traced is not None and start < traced.shape[1]:
            traced[:, pl.ds(start, width)] = jnp.maximum(
                traced[:, pl.ds(start, width)], jnp.max(scores, axis=0, keepdims=True)
            )
        for lane in range(0, width, 128):
            piece = scores[:, lane : lane + 128]
            best = piece if best is None else jnp.maximum(best, piece)
    return best


def over_lanes(best):
    return jnp.max(best.T, axis=0, keepdims=True)


def copies_in(refs, target, sems):
    height = refs[0].shape[0]
    copies = [
        pltpu.make_async_copy(ref, target.at[pl.ds(block * height, height)], sems.at[block])
        for block, ref in enumerate(refs)
    ]
    for copy in copies:
        copy.start()
    return copies


def tile_of(array, index, size):
    return array[pl.ds(pl.multiple_of(index * size, size), size), :]


def near_kernel(*refs):
    row_refs, col_refs = refs[:NEAR], refs[NEAR : NEAR + 3]
    lanes_out, rows, cols, row_sems, col_sems = refs[NEAR + 3 :]
    col_copies = copies_in(col_refs, cols, col_sems)
    copies_in(row_refs, rows, row_sems)
    for copy in col_copies:
        copy.wait()
    blocks = 3

    @pl.loop(0, NEAR // blocks)
    def _(index):
        for part in range(blocks):
            block = index * blocks + part
            pltpu.make_async_copy(row_refs[0], rows.at[pl.ds(block * SUB, SUB)], row_sems.at[block]).wait()
        size = blocks * SUB
        best = fold_chunks(None, tile_of(rows, index, size), cols, first_tile=index == 0)
        lanes_out[pl.ds(pl.multiple_of(index * size, size), size), :] = best


def mid_kernel(*refs):
    row_refs, col_refs = refs[:4], refs[4:7]
    _, _, lanes_out, rows_out, lanes, rows, cols, row_sems, col_sems, out_sems = refs[7:]
    for copy in copies_in(col_refs, cols, col_sems) + copies_in(row_refs, rows, row_sems):
        copy.wait()
    at = pl.ds(NEAR * SUB, PAIR)
    rows_copy = pltpu.make_async_copy(rows, rows_out.at[at], out_sems.at[0])
    rows_copy.start()
    lanes[...] = fold_chunks(None, rows[...], cols)
    lanes_copy = pltpu.make_async_copy(lanes, lanes_out.at[at], out_sems.at[1])
    lanes_copy.start()
    rows_copy.wait()
    lanes_copy.wait()


def last_kernel(after_ref, beside_before_ref, beside_across_ref, lanes, rows, best_out, col_out, cols, sems):
    copies = copies_in((after_ref, beside_before_ref, beside_across_ref), cols, sems)
    for copy in copies:
        copy.wait()
    col_out[...] = jnp.full(col_out.shape, -2.0, jnp.float32)
    best = over_lanes(fold_chunks(lanes[...], rows[...], cols, traced=col_out))
    for order, distance in enumerate((0, 3, 1, 2)):
        for core in range(2):
            begin = order * PAIR + core * SUB
            best_out[core, distance] = best[:, begin : begin + SUB]


ANYWHERE = pl.BlockSpec(memory_space=pl.ANY)
WHOLE = pl.BlockSpec(memory_space=pltpu.VMEM)


def run_kernel(kernel, out_shape, anywhere, whole, scratch, products, aliases=None):
    width = anywhere[0].shape[1]
    return pl.pallas_call(
        kernel,
        out_shape=out_shape,
        in_specs=[ANYWHERE] * len(anywhere) + [WHOLE] * len(whole),
        out_specs=[ANYWHERE if aliases else WHOLE] * len(out_shape),
        scratch_shapes=scratch,
        input_output_aliases=aliases or {},
        cost_estimate=pl.CostEstimate(
            flops=2 * products * SUB * SUB * width, bytes_accessed=products * SUB * width // 2, transcendentals=0
        ),
        compiler_params=pltpu.CompilerParams(vmem_limit_bytes=36 * 2**20),
    )(*anywhere, *whole)


def near_maxima(row_blocks, columns):
    width = columns[0].shape[1]
    total = len(row_blocks) * SUB + PAIR
    return run_kernel(
        near_kernel,
        [jax.ShapeDtypeStruct((total, 128), jnp.float32), jax.ShapeDtypeStruct((total, width), jnp.bfloat16)],
        [*row_blocks, *columns],
        [],
        [
            pltpu.VMEM((len(columns) * SUB, width), jnp.bfloat16),
            pltpu.SemaphoreType.DMA((len(row_blocks),)),
            pltpu.SemaphoreType.DMA((len(columns),)),
        ],
        len(row_blocks) * len(columns),
    )


def mid_maxima(row_blocks, columns, lanes, rows):
    width = columns[0].shape[1]
    count = len(row_blocks) + len(columns)
    return run_kernel(
        mid_kernel,
        [jax.ShapeDtypeStruct(lanes.shape, lanes.dtype), jax.ShapeDtypeStruct(rows.shape, rows.dtype)],
        [*row_blocks, *columns, lanes, rows],
        [],
        [
            pltpu.VMEM((PAIR, 128), jnp.float32),
            pltpu.VMEM((PAIR, width), jnp.bfloat16),
            pltpu.VMEM((len(columns) * SUB, width), jnp.bfloat16),
            pltpu.SemaphoreType.DMA((len(row_blocks),)),
            pltpu.SemaphoreType.DMA((len(columns),)),
            pltpu.SemaphoreType.DMA((2,)),
        ],
        2 * len(columns),
        {count: 0, count + 1: 1},
    )


def last_maxima(columns, lanes, rows):
    return run_kernel(
        last_kernel,
        [jax.ShapeDtypeStruct((2, 4, 1, SUB), jnp.float32), jax.ShapeDtypeStruct((1, PAIR), jnp.float32)],
        columns,
        [lanes, rows],
        [pltpu.VMEM((3 * SUB, rows.shape[1]), jnp.bfloat16), pltpu.SemaphoreType.DMA((3,))],
        24,
    )


def pack_kernel(capacity, owners, values_ref, rows_ref, send_ref, rows, picked, sem):
    copy = pltpu.make_async_copy(rows_ref, rows, sem)
    copy.start()
    lanes = lax.axis_size("tj")
    cluster = BLK * lax.axis_size("ti")
    count, features = rows.shape
    values = values_ref[...]
    member = values >= 0
    grp = jnp.where(values >= cluster, 1, 0)
    inside = values - grp * cluster - lax.axis_index("ti") * BLK
    part = jnp.zeros_like(inside)
    for step in range(1, lanes):
        part = part + jnp.where(inside >= step * SUB, 1, 0)
    code = inside - part * SUB + 1
    owner = jnp.where(member, grp * lanes + part, -1)
    owned = lax.broadcasted_iota(jnp.int32, (owners, count), 0) == owner
    owned_one = jnp.where(owned, 1.0, 0.0)
    block_shape = (BLOCK, BLOCK)
    before = lax.broadcasted_iota(jnp.int32, block_shape, 0) < lax.broadcasted_iota(jnp.int32, block_shape, 1)
    before = jnp.where(before, 1.0, 0.0).astype(jnp.bfloat16)
    so_far = jnp.zeros((owners, 1), jnp.float32)
    ranks = []
    for start in range(0, count, BLOCK):
        part_one = owned_one[:, start : start + BLOCK]
        ranks.append(jnp.dot(part_one.astype(jnp.bfloat16), before, preferred_element_type=jnp.float32) + so_far)
        so_far = so_far + jnp.sum(part_one, axis=1, keepdims=True)
    ranks = jnp.concatenate(ranks, axis=1)
    rank = jnp.sum(jnp.where(owned, ranks, 0.0), axis=0, keepdims=True).astype(jnp.int32)
    slot = jnp.where(member, owner * capacity + rank, -1)
    tag_at = lax.broadcasted_iota(jnp.int32, (TAGS, count), 0)
    low_part = code & 15
    tags = jnp.where(tag_at == 0, code - low_part, jnp.where(tag_at == 1, low_part, 0))
    tags = tags.astype(jnp.float32).astype(jnp.bfloat16)
    for start in range(0, owners * capacity, CHUNK):
        at = lax.broadcasted_iota(jnp.int32, (CHUNK, count), 0) + start
        picked[pl.ds(start, CHUNK), :] = jnp.where(at == slot, 1.0, 0.0).astype(jnp.bfloat16)
    places = lax.dot_general(picked[...], tags, (((1,), (1,)), ((), ())), preferred_element_type=jnp.float32)
    send_ref[:, features:] = places.astype(jnp.bfloat16)
    copy.wait()

    @pl.loop(0, features // CHUNK)
    def _(step):
        at = pl.ds(pl.multiple_of(step * CHUNK, CHUNK), CHUNK)
        taken = jnp.dot(picked[...], rows[:, at], preferred_element_type=jnp.float32)
        send_ref[:, at] = taken.astype(jnp.bfloat16)


def pack_rows(values, rows, capacity, owners):
    count, features = rows.shape
    return pl.pallas_call(
        functools.partial(pack_kernel, capacity, owners),
        out_shape=jax.ShapeDtypeStruct((owners * capacity, features + TAGS), jnp.bfloat16),
        in_specs=[WHOLE, ANYWHERE],
        out_specs=WHOLE,
        scratch_shapes=[
            pltpu.VMEM((count, features), jnp.bfloat16),
            pltpu.VMEM((owners * capacity, count), jnp.bfloat16),
            pltpu.SemaphoreType.DMA,
        ],
        cost_estimate=pl.CostEstimate(
            flops=2 * owners * capacity * count * features, bytes_accessed=4 * count * features, transcendentals=0
        ),
        compiler_params=pltpu.CompilerParams(vmem_limit_bytes=56 * 2**20),
    )(values, rows)


def per_device(corpus, slot_of_row):
    rows_in = corpus[0]
    src_count, features = rows_in.shape
    lanes = lax.axis_size("tj")
    sub_rows = src_count // 2
    capacity = BLK // (lanes * lanes)
    owners = 2 * lanes
    send = pack_rows(slot_of_row, rows_in, capacity, owners).reshape(owners, capacity, features + TAGS)
    got = lax.all_to_all(send, ("grp", "tj"), 0, 0, tiled=True).reshape(owners * capacity, features + TAGS)
    sum_tags = jnp.where(jnp.arange(TAGS, dtype=jnp.int32)[None, :] < 2, 1.0, 0.0).astype(jnp.bfloat16)
    got_places = lax.dot_general(
        sum_tags, got[:, features:], (((1,), (1,)), ((), ())), preferred_element_type=jnp.float32
    )
    wanted = jnp.arange(1, sub_rows + 1, dtype=jnp.int32)[:, None]
    place = (got_places.astype(jnp.int32) == wanted).astype(jnp.bfloat16)
    arrived = jnp.dot(place, got[:, :features], preferred_element_type=jnp.float32)
    row_squares = jnp.sum(arrived * arrived, axis=1, keepdims=True)
    own = (arrived * lax.rsqrt(row_squares + epsilon)).astype(jnp.bfloat16)

    def along_rows(value, pairs):
        return lax.ppermute(value, "ti", pairs)

    def along_cols(value, pairs):
        return lax.ppermute(value, "tj", pairs)

    size = lax.axis_size("ti")
    up = [(i, (i + 2) % size) for i in range(size)]
    down = [(i, (i - 2) % size) for i in range(size)]
    far = [(i, (i + 4) % size) for i in range(size)]
    swap = [(i, i ^ 1) for i in range(size)]
    twin = along_cols(own, swap)
    beside = along_rows(own, swap)
    across = along_rows(own, far)
    low = along_cols(own, up)
    high = along_cols(own, down)

    later, across = lax.optimization_barrier((own, across))
    low_twin = along_cols(low, swap)
    high_twin = along_cols(high, swap)
    half = sub_rows // 2
    low_half, high_half, low_twin, high_twin = lax.optimization_barrier((low[:half], high[half:], low_twin, high_twin))
    mid_top = along_cols(low_half, up)
    mid_bottom = along_cols(high_half, down)
    after = along_rows(later, down)
    beside_before = along_rows(beside, up)
    beside_across = along_rows(across, swap)

    lanes_best, rows = near_maxima([own, twin, low, low_twin, high, high_twin], [own, beside, across])
    mid_top, mid_bottom, lanes_best = lax.optimization_barrier((mid_top, mid_bottom, lanes_best))
    mid = [mid_top, mid_bottom, along_cols(mid_top, swap), along_cols(mid_bottom, swap)]
    lanes_best, rows = mid_maxima(mid, [own, beside, across], lanes_best, rows)
    row_best, col_best = last_maxima([after, beside_before, beside_across], lanes_best, rows)
    col_best = col_best.reshape(2, sub_rows)
    from_before = along_rows(col_best[:1], up)
    from_beside = along_rows(col_best[1:], [(i, ((i ^ 1) - 2) % size) for i in range(size)])
    twin_best = along_cols(row_best[1], swap)
    chip_best = jnp.maximum(row_best[0], twin_best)
    best = jnp.maximum(chip_best[0], jnp.maximum(from_before, from_beside))
    for step in range(1, lanes // 2):
        best = jnp.maximum(best, along_cols(chip_best[step], [(j, (j + 2 * step) % lanes) for j in range(lanes)]))
    return best


def solution(mesh):
    in_specs = (P("grp", ("ti", "tj"), None), P("grp", ("ti", "tj")))
    out_specs = P("grp", ("ti", "tj"))
    return jax.shard_map(
        per_device, mesh=mesh, in_specs=in_specs, out_specs=out_specs, check_vma=False
    )
```

```python
import functools

import jax
import jax.numpy as jnp
from jax import lax
from jax.experimental import pallas as pl
from jax.experimental.pallas import tpu as pltpu
from jax.sharding import PartitionSpec as P

BLK = 3072
SUB = 384
PAIR = 2 * SUB
CHUNK = 256
NEAR = 6
EARLY = 1024
TAGS = 128
epsilon = 1e-06


def score_chunk(row_tile, cols, start, width):
    return lax.dot_general(
        row_tile,
        cols[pl.ds(start, width), :],
        (((1,), (1,)), ((), ())),
        preferred_element_type=jnp.float32,
    )


def fold_chunks(best, row_tile, cols, traced=None, first_tile=None):
    total = cols.shape[0]
    for start in range(0, total, CHUNK):
        width = min(CHUNK, total - start)
        scores = score_chunk(row_tile, cols, start, width)
        if first_tile is not None and start < SUB:
            row_at = lax.broadcasted_iota(jnp.int32, scores.shape, 0)
            col_at = lax.broadcasted_iota(jnp.int32, scores.shape, 1) + start
            same = (row_at == col_at) & (col_at < SUB) & first_tile
            scores = jnp.where(same, -2.0, scores)
        if traced is not None and start < traced.shape[1]:
            traced[:, pl.ds(start, width)] = jnp.maximum(
                traced[:, pl.ds(start, width)], jnp.max(scores, axis=0, keepdims=True)
            )
        for lane in range(0, width, 128):
            piece = scores[:, lane : lane + 128]
            best = piece if best is None else jnp.maximum(best, piece)
    return best


def over_lanes(best):
    return jnp.max(best.T, axis=0, keepdims=True)


def copies_in(refs, target, sems):
    height = refs[0].shape[0]
    copies = [
        pltpu.make_async_copy(ref, target.at[pl.ds(block * height, height)], sems.at[block])
        for block, ref in enumerate(refs)
    ]
    for copy in copies:
        copy.start()
    return copies


def tile_of(array, index, size):
    return array[pl.ds(pl.multiple_of(index * size, size), size), :]


def near_kernel(*refs):
    row_refs, col_refs = refs[:NEAR], refs[NEAR : NEAR + 3]
    lanes_out, rows, cols, row_sems, col_sems = refs[NEAR + 3 :]
    col_copies = copies_in(col_refs, cols, col_sems)
    copies_in(row_refs, rows, row_sems)
    for copy in col_copies:
        copy.wait()
    blocks = 3

    @pl.loop(0, NEAR // blocks)
    def _(index):
        for part in range(blocks):
            block = index * blocks + part
            pltpu.make_async_copy(row_refs[0], rows.at[pl.ds(block * SUB, SUB)], row_sems.at[block]).wait()
        size = blocks * SUB
        best = fold_chunks(None, tile_of(rows, index, size), cols.at[pl.ds(0, EARLY)], first_tile=index == 0)
        lanes_out[pl.ds(pl.multiple_of(index * size, size), size), :] = best


def mid_kernel(*refs):
    row_refs, col_refs = refs[:4], refs[4:7]
    _, _, lanes_out, rows_out, lanes, rows, cols, row_sems, col_sems, out_sems = refs[7:]
    for copy in copies_in(col_refs, cols, col_sems) + copies_in(row_refs, rows, row_sems):
        copy.wait()
    at = pl.ds(NEAR * SUB, PAIR)
    rows_copy = pltpu.make_async_copy(rows, rows_out.at[at], out_sems.at[0])
    rows_copy.start()
    lanes[...] = fold_chunks(None, rows[...], cols.at[pl.ds(0, EARLY)])
    lanes_copy = pltpu.make_async_copy(lanes, lanes_out.at[at], out_sems.at[1])
    lanes_copy.start()
    rows_copy.wait()
    lanes_copy.wait()


def last_kernel(*refs):
    last_refs, first_ref = refs[:3], refs[3]
    lanes, rows, best_out, col_out, cols, sems = refs[4:]
    copies = copies_in(last_refs, cols, sems)
    rest = 3 * SUB - EARLY
    copies.append(
        pltpu.make_async_copy(first_ref.at[pl.ds(SUB - rest, rest)], cols.at[pl.ds(3 * SUB, rest)], sems.at[3])
    )
    copies[-1].start()
    for copy in copies:
        copy.wait()
    col_out[...] = jnp.full(col_out.shape, -2.0, jnp.float32)
    best = over_lanes(fold_chunks(lanes[...], rows[...], cols, traced=col_out))
    for order, distance in enumerate((0, 3, 1, 2)):
        for core in range(2):
            begin = order * PAIR + core * SUB
            best_out[core, distance] = best[:, begin : begin + SUB]


ANYWHERE = pl.BlockSpec(memory_space=pl.ANY)
WHOLE = pl.BlockSpec(memory_space=pltpu.VMEM)


def run_kernel(kernel, out_shape, anywhere, whole, scratch, products, aliases=None):
    width = anywhere[0].shape[1]
    return pl.pallas_call(
        kernel,
        out_shape=out_shape,
        in_specs=[ANYWHERE] * len(anywhere) + [WHOLE] * len(whole),
        out_specs=[ANYWHERE if aliases else WHOLE] * len(out_shape),
        scratch_shapes=scratch,
        input_output_aliases=aliases or {},
        cost_estimate=pl.CostEstimate(
            flops=2 * products * SUB * SUB * width, bytes_accessed=products * SUB * width // 2, transcendentals=0
        ),
        compiler_params=pltpu.CompilerParams(vmem_limit_bytes=36 * 2**20),
    )(*anywhere, *whole)


def near_maxima(row_blocks, columns):
    width = columns[0].shape[1]
    total = len(row_blocks) * SUB + PAIR
    return run_kernel(
        near_kernel,
        [jax.ShapeDtypeStruct((total, 128), jnp.float32), jax.ShapeDtypeStruct((total, width), jnp.bfloat16)],
        [*row_blocks, *columns],
        [],
        [
            pltpu.VMEM((len(columns) * SUB, width), jnp.bfloat16),
            pltpu.SemaphoreType.DMA((len(row_blocks),)),
            pltpu.SemaphoreType.DMA((len(columns),)),
        ],
        len(row_blocks) * len(columns),
    )


def mid_maxima(row_blocks, columns, lanes, rows):
    width = columns[0].shape[1]
    count = len(row_blocks) + len(columns)
    return run_kernel(
        mid_kernel,
        [jax.ShapeDtypeStruct(lanes.shape, lanes.dtype), jax.ShapeDtypeStruct(rows.shape, rows.dtype)],
        [*row_blocks, *columns, lanes, rows],
        [],
        [
            pltpu.VMEM((PAIR, 128), jnp.float32),
            pltpu.VMEM((PAIR, width), jnp.bfloat16),
            pltpu.VMEM((len(columns) * SUB, width), jnp.bfloat16),
            pltpu.SemaphoreType.DMA((len(row_blocks),)),
            pltpu.SemaphoreType.DMA((len(columns),)),
            pltpu.SemaphoreType.DMA((2,)),
        ],
        2 * len(columns),
        {count: 0, count + 1: 1},
    )


def last_maxima(columns, first_column, lanes, rows):
    return run_kernel(
        last_kernel,
        [jax.ShapeDtypeStruct((2, 4, 1, SUB), jnp.float32), jax.ShapeDtypeStruct((1, PAIR), jnp.float32)],
        [*columns, first_column],
        [lanes, rows],
        [pltpu.VMEM((6 * SUB - EARLY, rows.shape[1]), jnp.bfloat16), pltpu.SemaphoreType.DMA((4,))],
        24,
    )


def pack_kernel(capacity, owners, values_ref, rows_ref, send_ref, rows, picked, sem):
    copy = pltpu.make_async_copy(rows_ref, rows, sem)
    copy.start()
    lanes = lax.axis_size("tj")
    cluster = BLK * lax.axis_size("ti")
    count, features = rows.shape
    values = values_ref[...]
    member = values >= 0
    grp = jnp.where(values >= cluster, 1, 0)
    inside = values - grp * cluster - lax.axis_index("ti") * BLK
    part = jnp.zeros_like(inside)
    for step in range(1, lanes):
        part = part + jnp.where(inside >= step * SUB, 1, 0)
    code = inside - part * SUB + 1
    owner = jnp.where(member, grp * lanes + part, -1)
    owned = lax.broadcasted_iota(jnp.int32, (owners, count), 0) == owner
    square = (count, count)
    before = lax.broadcasted_iota(jnp.int32, square, 0) < lax.broadcasted_iota(jnp.int32, square, 1)
    before = jnp.where(before, 1.0, 0.0).astype(jnp.bfloat16)
    ranks = jnp.dot(jnp.where(owned, 1.0, 0.0).astype(jnp.bfloat16), before, preferred_element_type=jnp.float32)
    rank = jnp.sum(jnp.where(owned, ranks, 0.0), axis=0, keepdims=True).astype(jnp.int32)
    slot = jnp.where(member, owner * capacity + rank, -1)
    tag_at = lax.broadcasted_iota(jnp.int32, (TAGS, count), 0)
    low_part = code & 15
    tags = jnp.where(tag_at == 0, code - low_part, jnp.where(tag_at == 1, low_part, 0))
    tags = tags.astype(jnp.float32).astype(jnp.bfloat16)
    for start in range(0, owners * capacity, CHUNK):
        at = lax.broadcasted_iota(jnp.int32, (CHUNK, count), 0) + start
        picked[pl.ds(start, CHUNK), :] = jnp.where(at == slot, 1.0, 0.0).astype(jnp.bfloat16)
    places = lax.dot_general(picked[...], tags, (((1,), (1,)), ((), ())), preferred_element_type=jnp.float32)
    send_ref[:, features:] = places.astype(jnp.bfloat16)
    copy.wait()

    for start in range(0, features, CHUNK):
        taken = jnp.dot(picked[...], rows[:, pl.ds(start, CHUNK)], preferred_element_type=jnp.float32)
        send_ref[:, pl.ds(start, CHUNK)] = taken.astype(jnp.bfloat16)


def pack_rows(values, rows, capacity, owners):
    count, features = rows.shape
    return pl.pallas_call(
        functools.partial(pack_kernel, capacity, owners),
        out_shape=jax.ShapeDtypeStruct((owners * capacity, features + TAGS), jnp.bfloat16),
        in_specs=[WHOLE, ANYWHERE],
        out_specs=WHOLE,
        scratch_shapes=[
            pltpu.VMEM((count, features), jnp.bfloat16),
            pltpu.VMEM((owners * capacity, count), jnp.bfloat16),
            pltpu.SemaphoreType.DMA,
        ],
        cost_estimate=pl.CostEstimate(
            flops=2 * owners * capacity * count * features, bytes_accessed=4 * count * features, transcendentals=0
        ),
        compiler_params=pltpu.CompilerParams(vmem_limit_bytes=56 * 2**20),
    )(values, rows)


def per_device(corpus, slot_of_row):
    rows_in = corpus[0]
    src_count, features = rows_in.shape
    lanes = lax.axis_size("tj")
    sub_rows = src_count // 2
    capacity = BLK // (lanes * lanes)
    owners = 2 * lanes
    send = pack_rows(slot_of_row, rows_in, capacity, owners).reshape(owners, capacity, features + TAGS)
    got = lax.all_to_all(send, ("grp", "tj"), 0, 0, tiled=True).reshape(owners * capacity, features + TAGS)
    sum_tags = jnp.where(jnp.arange(TAGS, dtype=jnp.int32)[None, :] < 2, 1.0, 0.0).astype(jnp.bfloat16)
    got_places = lax.dot_general(
        sum_tags, got[:, features:], (((1,), (1,)), ((), ())), preferred_element_type=jnp.float32
    )
    wanted = jnp.arange(1, sub_rows + 1, dtype=jnp.int32)[:, None]
    place = (got_places.astype(jnp.int32) == wanted).astype(jnp.bfloat16)
    arrived = jnp.dot(place, got[:, :features], preferred_element_type=jnp.float32)
    row_squares = jnp.sum(arrived * arrived, axis=1, keepdims=True)
    own = (arrived * lax.rsqrt(row_squares + epsilon)).astype(jnp.bfloat16)

    def along_rows(value, pairs):
        return lax.ppermute(value, "ti", pairs)

    def along_cols(value, pairs):
        return lax.ppermute(value, "tj", pairs)

    size = lax.axis_size("ti")
    up = [(i, (i + 2) % size) for i in range(size)]
    down = [(i, (i - 2) % size) for i in range(size)]
    far = [(i, (i + 4) % size) for i in range(size)]
    swap = [(i, i ^ 1) for i in range(size)]
    twin = along_cols(own, swap)
    beside = along_rows(own, swap)
    across = along_rows(own, far)
    low = along_cols(own, up)
    high = along_cols(own, down)

    later, across = lax.optimization_barrier((own, across))
    low_twin = along_cols(low, swap)
    high_twin = along_cols(high, swap)
    half = sub_rows // 2
    low_half, high_half, low_twin, high_twin = lax.optimization_barrier((low[:half], high[half:], low_twin, high_twin))
    mid_top = along_cols(low_half, up)
    mid_bottom = along_cols(high_half, down)
    after = along_rows(later, down)
    beside_before = along_rows(beside, up)
    beside_across = along_rows(across, swap)

    lanes_best, rows = near_maxima([own, twin, low, low_twin, high, high_twin], [own, beside, across])
    mid_top, mid_bottom, lanes_best = lax.optimization_barrier((mid_top, mid_bottom, lanes_best))
    mid = [mid_top, mid_bottom, along_cols(mid_top, swap), along_cols(mid_bottom, swap)]
    lanes_best, rows = mid_maxima(mid, [own, beside, across], lanes_best, rows)
    row_best, col_best = last_maxima([after, beside_before, beside_across], across, lanes_best, rows)
    col_best = col_best.reshape(2, sub_rows)
    from_before = along_rows(col_best[:1], up)
    from_beside = along_rows(col_best[1:], [(i, ((i ^ 1) - 2) % size) for i in range(size)])
    twin_best = along_cols(row_best[1], swap)
    chip_best = jnp.maximum(row_best[0], twin_best)
    best = jnp.maximum(chip_best[0], jnp.maximum(from_before, from_beside))
    for step in range(1, lanes // 2):
        best = jnp.maximum(best, along_cols(chip_best[step], [(j, (j + 2 * step) % lanes) for j in range(lanes)]))
    return best


def solution(mesh):
    in_specs = (P("grp", ("ti", "tj"), None), P("grp", ("ti", "tj")))
    out_specs = P("grp", ("ti", "tj"))
    return jax.shard_map(
        per_device, mesh=mesh, in_specs=in_specs, out_specs=out_specs, check_vma=False
    )
```
